512 devices in a mesh: dp: 2 (over x_lo), segment: 16 (over x_hi, y, core), space: 16 (over z).
Axes of the slice: x: 4 (x_hi: 2, x_lo: 2; x = x_hi * 2 + x_lo), y: 4, z: 16, core: 2. Of those that a mesh axis runs over, the one named last changes fastest.
Arguments:
- features: bfloat16 [2, 16, 32, 96, 6, 256], P('dp', 'segment', None, 'space'), may hold values from -6 to 6
- out_grad: bfloat16 [2, 16, 64, 48, 3, 128], P('dp', 'segment', None, 'space'), may hold values from -6 to 6
- weight_mean: float32 [16, 27, 2048], P('segment'), may hold values from -0.21875 to 0.21875
- weight_noise: float32 [16, 27, 2048], P('segment'), may hold values from -4 to 4
- precision: float32 [16, 27, 2048], P('segment'), may hold values from 0.5 to 4
Outputs:
- act_in: bfloat16 [2, 16, 64, 48, 3, 128], P('dp', 'segment', None, 'space')
- grad_in: bfloat16 [2, 16, 32, 96, 6, 256], P('dp', 'segment', None, 'space')
- mean_next: float32 [16, 27, 2048], P('segment')
- precision_next: float32 [16, 27, 2048], P('segment')
The draws below stay inside these ranges and needn't reach their ends.
All inputs are finite; a program needn't handle non-finite values.
Results may differ from the reference program's by a relative error of at most 0.007.
Values may be sent and summed in bfloat16 or wider, within the bound.
A program may use at most 64 MiB of HBM per device.

```python
import math
import jax
import jax.numpy as jnp
from jax import lax

CIN = 32
COUT = 64
XD = 6
YS = 6
ZS = 256
N_DP = 2
N_SEGMENT = 16
N_SPACE = 16


def level_of(stream_key, shape, shards, low, largest):
    gain, own = 1.0, jax.random.fold_in(stream_key, 6)
    for dim, shards_of in shards:
        steps = jnp.exp(jax.random.uniform(jax.random.fold_in(own, dim), (shards_of,), jnp.float32, low / len(shards), largest / len(shards)))
        gain = gain * jnp.repeat(steps, shape[dim] // shards_of).reshape([-1 if axis == dim else 1 for axis in range(len(shape))])
    return gain


def normal_values(key, extent, width, reach, split=(), dtype=jnp.bfloat16):
    loudness = level_of(key, extent, split, -0.22, 0.18) if split else 1.0
    values = jax.random.normal(key, extent, jnp.float32) * width * loudness
    return jnp.minimum(jnp.maximum(values, -reach), reach).astype(dtype)


def setup_inputs(seed: int = 0) -> dict:
    splits = jax.random.split(jax.random.key(seed), 6)
    return {
        "features": normal_values(splits[0], (N_DP, N_SEGMENT, CIN, XD * N_SPACE, YS, ZS), 1.0, 6.0, ((0, 2), (1, 16), (3, 16))),
        "out_grad": normal_values(splits[1], (N_DP, N_SEGMENT, COUT, XD // 2 * N_SPACE, YS // 2, ZS // 2), 1.0, 6.0, ((0, 2), (1, 16), (3, 16))),
        "weight_mean": normal_values(splits[2], (N_SEGMENT, 27, COUT * CIN), (27 * CIN) ** -0.5, 0.21875, ((0, 16),), jnp.float32),
        "weight_noise": normal_values(splits[3], (N_SEGMENT, 27, COUT * CIN), 1.0, 4.0, ((0, 16),), jnp.float32),
        "precision": jnp.clip(jnp.exp(math.log(4.0) - 2.0794415 * jax.random.uniform(splits[4], (N_SEGMENT, 27, COUT * CIN), jnp.float32) ** level_of(splits[4], (N_SEGMENT, 27, COUT * CIN), ((0, 16),), -0.2, 0.2)), 0.5, 4.0),
    }


CONV_LAYOUT = ('NCDHW', 'OIDHW', 'NCDHW')

def noisy_weights(weight_mean, weight_noise, precision, cout, cin):
    noisy = weight_mean + weight_noise * lax.rsqrt(2000.0 * (precision + 0.1))
    kernel = noisy.astype(jnp.bfloat16).reshape(3, 3, 3, cout, cin)
    return jnp.transpose(kernel, (3, 4, 0, 1, 2))

def forward_conv(padded, kernel):
    return lax.conv_general_dilated(padded[None], kernel, (2, 2, 2), 'VALID', dimension_numbers=CONV_LAYOUT, preferred_element_type=jnp.float32)[0]

def input_conv(pre_grad, kernel):
    flipped = jnp.transpose(kernel[:, :, ::-1, ::-1, ::-1], (1, 0, 2, 3, 4))
    return lax.conv_general_dilated(pre_grad[None], flipped, (1, 1, 1), ((2, 2), (2, 2), (2, 2)), lhs_dilation=(2, 2, 2), dimension_numbers=CONV_LAYOUT, preferred_element_type=jnp.float32)[0]

def weight_conv(padded, pre_grad):
    grads = lax.conv_general_dilated(padded[:, None], pre_grad[:, None], (1, 1, 1), 'VALID', rhs_dilation=(2, 2, 2), dimension_numbers=CONV_LAYOUT, preferred_element_type=jnp.float32)
    return jnp.transpose(grads, (2, 3, 4, 1, 0)).reshape(27, -1)

def reference(features, out_grad, weight_mean, weight_noise, precision):
    cell_count = N_DP * N_SPACE * (XD // 2) * (YS // 2) * (ZS // 2)
    inv_root = 1.0 / math.sqrt(cell_count)

    def per_segment(segment_item):
        feats, grads, mean, noise, prec = segment_item
        kernel = noisy_weights(mean, noise, prec, COUT, CIN)
        outputs = []
        input_grads = []
        grad_total = jnp.zeros((27, COUT * CIN), jnp.float32)
        for replica in range(N_DP):
            padded = jnp.pad(feats[replica], ((0, 0), (1, 0), (1, 0), (1, 0)))
            preact = forward_conv(padded, kernel)
            outputs.append(jax.nn.silu(preact).astype(jnp.bfloat16))
            squash = jax.nn.sigmoid(preact)
            pre_grad = (grads[replica].astype(jnp.float32) * squash * (1.0 + preact * (1.0 - squash))).astype(jnp.bfloat16)
            spread_grad = input_conv(pre_grad, kernel)
            input_grads.append(spread_grad[:, 1:, 1:, 1:])
            grad_total = grad_total + weight_conv(padded, pre_grad)
        scaled = grad_total * inv_root
        prec_next = 0.75 * prec + 0.25 * scaled * scaled
        mean_new = mean - 0.03 * scaled / (prec_next + 0.1)
        return (jnp.stack(outputs), jnp.stack(input_grads).astype(jnp.bfloat16), mean_new, prec_next)
    outputs, input_grads, mean_next, precision_next = lax.map(per_segment, (jnp.swapaxes(features, 0, 1), jnp.swapaxes(out_grad, 0, 1), weight_mean, weight_noise, precision))
    outputs = jnp.swapaxes(outputs, 0, 1)
    input_grads = jnp.swapaxes(input_grads, 0, 1)
    act_in = jnp.concatenate([jnp.zeros_like(outputs[:, :1]), outputs[:, :-1]], axis=1)
    grad_in = jnp.concatenate([input_grads[:, 1:], jnp.zeros_like(input_grads[:, :1])], axis=1)
    return (act_in, grad_in, mean_next, precision_next)
```

```python
import functools
import math

import jax
import jax.numpy as jnp
from jax import lax
from jax.experimental import pallas as pl
from jax.experimental.pallas import tpu as pltpu
from jax.sharding import PartitionSpec as P

MESH = pl.DeviceIdType.MESH
BF16, F32 = jnp.bfloat16, jnp.float32
TAPS = 27
GROUPS = 7


def matmul(a, b, contract=((1,), (0,))):
    return lax.dot_general(a, b, (contract, ((), ())), preferred_element_type=F32)


def kernel(
    n_dp, n_seg, n_space, per_owner,
    feats, og, mean, noise, prec,
    act_out, gin_out, mean_out, prec_out,
    cells, wts, wtr, l_own, l_got, halo, act_own, act_got, pg_own, pg_got, shifted,
    grads, tiles, rs_got, total, ag_got,
    p_send, p_recv, rs_send, rs_recv, ag_send, ag_recv,
):
    dp, seg, space = (lax.axis_index(a) for a in ("dp", "segment", "space"))
    n_group = n_dp * n_space
    owners = -(-TAPS // per_owner)
    me = dp * n_space + space
    first_seg, last_seg = seg == 0, seg == n_seg - 1
    has_next, has_prev = seg < n_seg - 1, seg > 0
    has_up, has_down = space < n_space - 1, space > 0

    def at(d, s, z):
        return {"dp": d, "segment": s, "space": z}

    def peer(k):
        other = lax.rem(me + k, n_group)
        return other, at(other // n_space, seg, lax.rem(other, n_space))

    barrier = pltpu.get_barrier_semaphore()

    def greet(k, carry):
        pl.semaphore_signal(barrier, inc=1, device_id=peer(k)[1], device_id_type=MESH)
        return carry

    lax.fori_loop(1, n_group, greet, 0)
    for cond, to in (
        (has_prev, at(dp, seg - 1, space)),
        (has_next, at(dp, seg + 1, space)),
        (has_prev & has_down, at(dp, seg - 1, space - 1)),
        (has_next & has_up, at(dp, seg + 1, space + 1)),
    ):
        @pl.when(cond)
        def _():
            pl.semaphore_signal(barrier, inc=1, device_id=to, device_id_type=MESH)

    def link(i, src, dst, to):
        return pltpu.make_async_remote_copy(
            src_ref=src, dst_ref=dst, send_sem=p_send.at[i], recv_sem=p_recv.at[i],
            device_id=to, device_id_type=MESH,
        )

    prev = at(dp, seg - 1, space)
    after = at(dp, seg + 1, space)
    links = [
        (link(0, feats.at[feats.shape[0] - 1], halo, at(dp, seg, space + 1)), has_up, has_down),
        (link(1, l_own, l_got, prev), has_prev, has_next),
        (link(2, act_own.at[pl.ds(1, 2)], act_got.at[pl.ds(1, 2)], after), has_next, has_prev),
        (link(3, act_own.at[0], act_got.at[0], after), has_next, has_prev),
        (link(4, pg_own.at[pl.ds(1, 2)], pg_got.at[pl.ds(1, 2)], prev), has_prev, has_next),
        (link(5, pg_own.at[0], pg_got.at[0], prev), has_prev, has_next),
        (
            link(6, pg_own.at[0], pg_got.at[3], at(dp, seg - 1, space - 1)),
            has_prev & has_down,
            has_next & has_up,
        ),
    ]

    def start(i):
        copy, sends, _ = links[i]

        @pl.when(sends)
        def _():
            copy.start()

    def arrived(i):
        copy, _, receives = links[i]

        @pl.when(receives)
        def _():
            copy.wait_recv()

    def sent(i):
        copy, sends, _ = links[i]

        @pl.when(sends)
        def _():
            copy.wait_send()

    lane = lax.broadcasted_iota(jnp.int32, (16, 128), 1)
    chunk = lane // 32

    slabs = []
    for t in range(TAPS):
        rows = pl.ds(16 * t, 16)
        slabs.append(mean[rows] + noise[rows] * lax.rsqrt(2000.0 * (prec[rows] + 0.1)))
    for g in range(GROUPS):
        for low in range(4):
            block = jnp.zeros((16, 128), F32)
            for tl in range(4):
                if 4 * g + tl < TAPS:
                    turned = slabs[4 * g + tl]
                    if tl != low:
                        turned = pltpu.roll(turned, ((tl - low) * 32) % 128, 1)
                    block = jnp.where(chunk == tl, turned, block)
            wts[g, pl.ds(low, 16, stride=4), :] = block

    peers = (
        n_group - 1
        + has_prev.astype(jnp.int32)
        + has_next.astype(jnp.int32)
        + (has_prev & has_down).astype(jnp.int32)
        + (has_next & has_up).astype(jnp.int32)
    )
    pl.semaphore_wait(barrier, peers)
    start(0)

    z_of = lax.broadcasted_iota(jnp.int32, (256, 384), 0)
    column = lax.broadcasted_iota(jnp.int32, (256, 384), 1)
    pick = (z_of == 2 * (column % 128) + column // 128 - 1).astype(F32).astype(BF16)

    def spread(plane, x):
        got = matmul(plane.reshape(192, 256), pick).astype(BF16)
        for y in range(6):
            for e in range(3):
                cells[x, y + 1, pl.ds(32 * e, 32), :] = got[
                    32 * y : 32 * y + 32, 128 * e : 128 * e + 128
                ]

    for x in range(7):
        cells[x, 0] = jnp.zeros((96, 128), BF16)

    def patch(i):
        blocks = []
        for j in range(3):
            parts = [cells[2 * i + a, 2 * j : 2 * j + 3].reshape(288, 128) for a in range(3)]
            blocks.append(jnp.concatenate([*parts, jnp.zeros((32, 128), BF16)], axis=0))
        return jnp.concatenate(blocks, axis=1)

    def forward(i, weights):
        preact = matmul(weights, patch(i))
        grad = jnp.concatenate([og[i, j] for j in range(3)], axis=1).astype(F32)
        gate = jax.nn.sigmoid(preact)
        act = (preact * gate).astype(BF16)
        pre_grad = (grad * gate * (1.0 + preact * (1.0 - gate))).astype(BF16)
        for j in range(3):
            act_own[i, j] = act[:, 128 * j : 128 * j + 128]
            pg_own[i, j] = pre_grad[:, 128 * j : 128 * j + 128]

    def flat_weights():
        return jnp.concatenate([wts[g] for g in range(GROUPS)], axis=1).astype(BF16)

    for x in range(6):
        spread(feats[x], x + 1)
    for i in (1, 2):
        forward(i, flat_weights())
    start(2)
    start(4)

    for g in range(GROUPS):
        wtr[pl.ds(128 * g, 128), :] = jnp.concatenate([wts[g], wts[g]], axis=0).T
    half = lax.broadcasted_iota(jnp.int32, (32, 128), 1) < 64
    for ab in range(9):
        w0, w1, w2 = (wtr[pl.ds(32 * (3 * ab + e), 32), :] for e in range(3))
        even = jnp.where(half, w1, 0.0)
        odd = jnp.where(half, w2, w0)
        l_own[ab] = jnp.concatenate([even, odd], axis=0).astype(BF16)
    start(1)

    @pl.when(has_down)
    def _():
        arrived(0)
        spread(halo[...], 0)

    @pl.when(jnp.logical_not(has_down))
    def _():
        cells[0] = jnp.zeros(cells.shape[1:], BF16)

    forward(0, flat_weights())
    for i in (3, 5, 6):
        start(i)

    for i in (1, 2, 0):
        pre_grad = jnp.concatenate([pg_own[i, j] for j in range(3)], axis=1)
        part = matmul(pre_grad, patch(i), ((1,), (1,)))
        for g in range(GROUPS):
            piece = part[:, 128 * g : 128 * g + 128]
            grads[g] = piece if i == 1 else grads[g] + piece
    for g in range(GROUPS):
        rows = [grads[g, pl.ds(low, 16, stride=4), :] for low in range(4)]
        for tl in range(4):
            t = 4 * g + tl
            if t < TAPS:
                tile = jnp.zeros((16, 128), F32)
                for low in range(4):
                    turned = rows[low]
                    if tl != low:
                        turned = pltpu.roll(turned, ((low - tl) * 32) % 128, 1)
                    tile = jnp.where(chunk == low, turned, tile)
                tiles[t] = tile.astype(BF16)
    for t in range(TAPS, tiles.shape[0]):
        tiles[t] = jnp.zeros((16, 128), BF16)

    def rs_copy(other, to):
        return pltpu.make_async_remote_copy(
            src_ref=tiles.at[pl.ds(other * per_owner, per_owner)], dst_ref=rs_got.at[me],
            send_sem=rs_send.at[other], recv_sem=rs_recv.at[me],
            device_id=to, device_id_type=MESH,
        )

    def rs_arrival(other):
        return pltpu.make_async_remote_copy(
            src_ref=tiles.at[pl.ds(0, per_owner)], dst_ref=rs_got.at[other],
            send_sem=rs_send.at[other], recv_sem=rs_recv.at[other],
            device_id=at(dp, seg, space), device_id_type=MESH,
        )

    def rs_go(k, carry):
        other, to = peer(k)

        @pl.when(other < owners)
        def _():
            rs_copy(other, to).start()

        return carry

    lax.fori_loop(1, n_group, rs_go, 0)

    for i in (2, 3):
        arrived(i)

    @pl.when(has_prev)
    def _():
        act_out[...] = act_got[...]

    @pl.when(first_seg)
    def _():
        act_out[...] = jnp.zeros(act_out.shape, BF16)

    def planes(which, l_rows):
        put_r = lax.broadcasted_iota(jnp.int32, (256, 256), 0)
        put_c = lax.broadcasted_iota(jnp.int32, (256, 256), 1)
        weave = (put_c == 2 * (put_r % 128) + put_r // 128).astype(F32).astype(BF16)
        for i, pp in which:
            rows_i = [(1, i)] if pp == 0 else [(2, i), (0, i + 1)]
            lines = [None] * 6
            for qq in range(2):
                cols_j = [(1, 0)] if qq == 0 else [(2, 0), (0, 1)]
                left = jnp.concatenate(
                    [l_rows[3 * a + b] for a, _ in rows_i for b, _ in cols_j], axis=1
                )
                right = jnp.concatenate(
                    [
                        jnp.concatenate(
                            [shifted[ii, j + dj] for _, ii in rows_i for _, dj in cols_j], axis=0
                        )
                        for j in range(3)
                    ],
                    axis=1,
                )
                got = matmul(left, right).astype(BF16)
                for j in range(3):
                    line = got[:, 128 * j : 128 * j + 128]
                    lines[2 * j + qq] = jnp.concatenate([line[:32], line[32:]], axis=1)
            plane = matmul(jnp.concatenate(lines, axis=0), weave).astype(BF16)
            gin_out[2 * i + pp] = plane.reshape(6, 32, 256)

    inside = lax.broadcasted_iota(jnp.int32, (64, 128), 1) < 127

    def shift(i):
        for j in range(3):
            here = pg_got[i, j]
            moved = jnp.where(inside, pltpu.roll(here.astype(F32), 127, 1), 0.0)
            shifted[i, j, pl.ds(0, 64), :] = here
            shifted[i, j, pl.ds(64, 64), :] = moved.astype(BF16)
        shifted[i, 3] = jnp.zeros((128, 128), BF16)

    arrived(1)
    arrived(4)
    arrived(5)
    arrived(6)

    @pl.when(has_next)
    def _():
        @pl.when(jnp.logical_not(has_up))
        def _():
            pg_got[3] = jnp.zeros(pg_got.shape[1:], BF16)

        for i in range(4):
            shift(i)
        planes([(0, 0), (0, 1), (1, 0), (1, 1), (2, 0), (2, 1)], l_got)

    @pl.when(last_seg)
    def _():
        gin_out[...] = jnp.zeros(gin_out.shape, BF16)

    def ag_copy(other, to):
        return pltpu.make_async_remote_copy(
            src_ref=total, dst_ref=ag_got.at[pl.ds(me * per_owner, per_owner)],
            send_sem=ag_send.at[other], recv_sem=ag_recv.at[me],
            device_id=to, device_id_type=MESH,
        )

    def ag_arrival(other):
        return pltpu.make_async_remote_copy(
            src_ref=total, dst_ref=ag_got.at[pl.ds(other * per_owner, per_owner)],
            send_sem=ag_send.at[other], recv_sem=ag_recv.at[other],
            device_id=at(dp, seg, space), device_id_type=MESH,
        )

    inv_root = 1.0 / math.sqrt(n_group * 3 * 3 * 128)

    @pl.when(me < owners)
    def _():
        rs_got[me] = tiles[pl.ds(me * per_owner, per_owner)]

        def rs_wait(k, carry):
            rs_arrival(peer(k)[0]).wait_recv()
            return carry

        lax.fori_loop(1, n_group, rs_wait, 0)
        summed = rs_got[0].astype(F32)
        for k in range(1, n_group):
            summed += rs_got[k].astype(F32)
        total[...] = (summed * inv_root).astype(BF16)

        def ag_go(k, carry):
            other, to = peer(k)
            ag_copy(other, to).start()
            return carry

        lax.fori_loop(1, n_group, ag_go, 0)
        ag_got[pl.ds(me * per_owner, per_owner)] = total[...]

    def ag_wait(k, carry):
        other, _ = peer(k)

        @pl.when(other < owners)
        def _():
            ag_arrival(other).wait_recv()

        return carry

    lax.fori_loop(1, n_group, ag_wait, 0)
    for t in range(TAPS):
        rows = pl.ds(16 * t, 16)
        scaled = ag_got[t].astype(F32)
        prec_new = 0.75 * prec[rows] + 0.25 * scaled * scaled
        prec_out[rows] = prec_new
        mean_out[rows] = mean[rows] - 0.03 * scaled / (prec_new + 0.1)

    for i in range(len(links)):
        sent(i)

    def rs_sent(k, carry):
        other, to = peer(k)

        @pl.when(other < owners)
        def _():
            rs_copy(other, to).wait_send()

        @pl.when(me < owners)
        def _():
            ag_copy(other, to).wait_send()

        return carry

    lax.fori_loop(1, n_group, rs_sent, 0)


def per_device(features, out_grad, weight_mean, weight_noise, precision):
    n_dp, n_seg, n_space = (lax.axis_size(a) for a in ("dp", "segment", "space"))
    n_group = n_dp * n_space
    per_owner = -(-TAPS // n_group)
    feats = jnp.transpose(features[0, 0], (1, 2, 0, 3))
    og = jnp.transpose(out_grad[0, 0], (1, 2, 0, 3))
    mean, noise, prec = (
        w.reshape(TAPS * 16, 128) for w in (weight_mean, weight_noise, precision)
    )
    vmem = pl.BlockSpec(memory_space=pltpu.VMEM)
    act, gin, mean_new, prec_new = pl.pallas_call(
        functools.partial(kernel, n_dp, n_seg, n_space, per_owner),
        out_shape=[
            jax.ShapeDtypeStruct((3, 3, 64, 128), BF16),
            jax.ShapeDtypeStruct((6, 6, 32, 256), BF16),
            jax.ShapeDtypeStruct((TAPS * 16, 128), F32),
            jax.ShapeDtypeStruct((TAPS * 16, 128), F32),
        ],
        in_specs=[vmem] * 5,
        out_specs=[vmem] * 4,
        scratch_shapes=[
            pltpu.VMEM((7, 7, 96, 128), BF16),
            pltpu.VMEM((GROUPS, 64, 128), F32),
            pltpu.VMEM((GROUPS * 128, 128), F32),
            pltpu.VMEM((9, 64, 128), BF16),
            pltpu.VMEM((9, 64, 128), BF16),
            pltpu.VMEM((6, 32, 256), BF16),
            pltpu.VMEM((3, 3, 64, 128), BF16),
            pltpu.VMEM((3, 3, 64, 128), BF16),
            pltpu.VMEM((3, 3, 64, 128), BF16),
            pltpu.VMEM((4, 3, 64, 128), BF16),
            pltpu.VMEM((4, 4, 128, 128), BF16),
            pltpu.VMEM((GROUPS, 64, 128), F32),
            pltpu.VMEM((n_group * per_owner, 16, 128), BF16),
            pltpu.VMEM((n_group, per_owner, 16, 128), BF16),
            pltpu.VMEM((per_owner, 16, 128), BF16),
            pltpu.VMEM((n_group * per_owner, 16, 128), BF16),
            pltpu.SemaphoreType.DMA((7,)),
            pltpu.SemaphoreType.DMA((7,)),
            pltpu.SemaphoreType.DMA((n_group,)),
            pltpu.SemaphoreType.DMA((n_group,)),
            pltpu.SemaphoreType.DMA((n_group,)),
            pltpu.SemaphoreType.DMA((n_group,)),
        ],
        compiler_params=pltpu.CompilerParams(
            collective_id=0, has_side_effects=True, vmem_limit_bytes=40 * 2**20
        ),
        cost_estimate=pl.CostEstimate(
            flops=600_000_000, bytes_accessed=3_000_000, transcendentals=200_000
        ),
    )(feats, og, mean, noise, prec)
    act = jnp.transpose(act, (2, 0, 1, 3))
    gin = jnp.transpose(gin, (2, 0, 1, 3))
    return (
        act[None, None],
        gin[None, None],
        mean_new.reshape(1, TAPS, 2048),
        prec_new.reshape(1, TAPS, 2048),
    )


def solution(mesh):
    in_specs = (
        P("dp", "segment", None, "space", None, None),
        P("dp", "segment", None, "space", None, None),
        P("segment", None, None),
        P("segment", None, None),
        P("segment", None, None),
    )
    out_specs = (
        P("dp", "segment", None, "space", None, None),
        P("dp", "segment", None, "space", None, None),
        P("segment", None, None),
        P("segment", None, None),
    )
    return jax.shard_map(
        per_device, mesh=mesh, in_specs=in_specs, out_specs=out_specs, check_vma=False
    )
```

```python
import functools
import math

import jax
import jax.numpy as jnp
from jax import lax
from jax.experimental import pallas as pl
from jax.experimental.pallas import tpu as pltpu
from jax.sharding import PartitionSpec as P

MESH = pl.DeviceIdType.MESH
BF16, F32 = jnp.bfloat16, jnp.float32
TAPS = 27
GROUPS = 7


def matmul(a, b, contract=((1,), (0,))):
    return lax.dot_general(a, b, (contract, ((), ())), preferred_element_type=F32)


def kernel(
    n_dp, n_seg, n_space, near, share,
    feats_hbm, og_hbm, mean_hbm, noise_hbm, prec_hbm,
    act_out, gin_out, mean_out, prec_out,
    feats, og, mean, noise, prec,
    cells, wts, wtr, l_own, l_got, halo, act_own, act_got, pg_own, pg_got, shifted,
    grads, tiles, rs_got, far_got, total, ag_got,
    loaded, p_send, p_recv, rs_send, rs_recv, far_send, far_recv, ag_send, ag_recv,
):
    dp, seg, space = (lax.axis_index(a) for a in ("dp", "segment", "space"))
    n_near, n_far = n_dp * near, n_space // near
    owners = -(-TAPS // share)
    spot, band = lax.rem(space, near), space // near
    me = dp * near + spot
    first_seg, last_seg = seg == 0, seg == n_seg - 1
    has_next, has_prev = seg < n_seg - 1, seg > 0
    has_up, has_down = space < n_space - 1, space > 0

    def at(d, s, z):
        return {"dp": d, "segment": s, "space": z}

    def peer(k):
        other = lax.rem(me + k, n_near)
        return other, at(other // near, seg, band * near + lax.rem(other, near))

    def far_peer(k):
        other = lax.rem(band + k, n_far)
        return other, at(dp, seg, other * near + spot)

    barrier = pltpu.get_barrier_semaphore()
    greeted = [(True, peer(k)[1]) for k in range(1, n_near)]
    greeted += [(True, far_peer(k)[1]) for k in range(1, n_far)]
    greeted += [
        (has_down & (spot == 0), at(dp, seg, space - 1)),
        (has_up & (spot == near - 1), at(dp, seg, space + 1)),
        (has_prev, at(dp, seg - 1, space)),
        (has_next, at(dp, seg + 1, space)),
        (has_prev & has_down, at(dp, seg - 1, space - 1)),
        (has_next & has_up, at(dp, seg + 1, space + 1)),
    ]
    peers = 0
    for cond, to in greeted:
        if cond is True:
            pl.semaphore_signal(barrier, inc=1, device_id=to, device_id_type=MESH)
            peers = peers + 1
        else:
            @pl.when(cond)
            def _():
                pl.semaphore_signal(barrier, inc=1, device_id=to, device_id_type=MESH)

            peers = peers + cond.astype(jnp.int32)

    loads = [
        pltpu.make_async_copy(src, dst, loaded.at[i])
        for i, (src, dst) in enumerate(
            [(mean_hbm, mean), (noise_hbm, noise), (prec_hbm, prec), (feats_hbm, feats), (og_hbm, og)]
        )
    ]
    for load in loads:
        load.start()
    pl.semaphore_wait(barrier, peers)

    def link(i, src, dst, to):
        return pltpu.make_async_remote_copy(
            src_ref=src, dst_ref=dst, send_sem=p_send.at[i], recv_sem=p_recv.at[i],
            device_id=to, device_id_type=MESH,
        )

    prev = at(dp, seg - 1, space)
    after = at(dp, seg + 1, space)
    links = [
        (link(0, feats_hbm.at[feats_hbm.shape[0] - 1], halo, at(dp, seg, space + 1)), has_up, has_down),
        (link(1, l_own, l_got, prev), has_prev, has_next),
        (link(2, act_own.at[pl.ds(1, 2)], act_got.at[pl.ds(1, 2)], after), has_next, has_prev),
        (link(3, act_own.at[0], act_got.at[0], after), has_next, has_prev),
        (link(4, pg_own.at[pl.ds(1, 2)], pg_got.at[pl.ds(1, 2)], prev), has_prev, has_next),
        (link(5, pg_own.at[0], pg_got.at[0], prev), has_prev, has_next),
        (
            link(6, pg_own.at[0], pg_got.at[3], at(dp, seg - 1, space - 1)),
            has_prev & has_down,
            has_next & has_up,
        ),
    ]

    def start(i):
        copy, sends, _ = links[i]

        @pl.when(sends)
        def _():
            copy.start()

    def arrived(i):
        copy, _, receives = links[i]

        @pl.when(receives)
        def _():
            copy.wait_recv()

    def sent(i):
        copy, sends, _ = links[i]

        @pl.when(sends)
        def _():
            copy.wait_send()

    start(0)
    lane = lax.broadcasted_iota(jnp.int32, (16, 128), 1)
    chunk = lane // 32

    for load in loads[:3]:
        load.wait()
    slabs = []
    for t in range(TAPS):
        rows = pl.ds(16 * t, 16)
        slabs.append(mean[rows] + noise[rows] * lax.rsqrt(2000.0 * (prec[rows] + 0.1)))
    for g in range(GROUPS):
        for low in range(4):
            block = jnp.zeros((16, 128), F32)
            for tl in range(4):
                if 4 * g + tl < TAPS:
                    turned = slabs[4 * g + tl]
                    if tl != low:
                        turned = pltpu.roll(turned, ((tl - low) * 32) % 128, 1)
                    block = jnp.where(chunk == tl, turned, block)
            wts[g, pl.ds(low, 16, stride=4), :] = block

    z_of = lax.broadcasted_iota(jnp.int32, (256, 384), 0)
    column = lax.broadcasted_iota(jnp.int32, (256, 384), 1)
    pick = (z_of == 2 * (column % 128) + column // 128 - 1).astype(F32).astype(BF16)

    def spread(plane, x):
        got = matmul(plane.reshape(192, 256), pick).astype(BF16)
        for y in range(6):
            for e in range(3):
                cells[x, y + 1, pl.ds(32 * e, 32), :] = got[
                    32 * y : 32 * y + 32, 128 * e : 128 * e + 128
                ]

    for x in range(7):
        cells[x, 0] = jnp.zeros((96, 128), BF16)

    def patch(i):
        blocks = []
        for j in range(3):
            parts = [cells[2 * i + a, 2 * j : 2 * j + 3].reshape(288, 128) for a in range(3)]
            blocks.append(jnp.concatenate([*parts, jnp.zeros((32, 128), BF16)], axis=0))
        return jnp.concatenate(blocks, axis=1)

    def forward(i, weights):
        preact = matmul(weights, patch(i))
        grad = jnp.concatenate([og[i, j] for j in range(3)], axis=1).astype(F32)
        gate = jax.nn.sigmoid(preact)
        act = (preact * gate).astype(BF16)
        pre_grad = (grad * gate * (1.0 + preact * (1.0 - gate))).astype(BF16)
        for j in range(3):
            act_own[i, j] = act[:, 128 * j : 128 * j + 128]
            pg_own[i, j] = pre_grad[:, 128 * j : 128 * j + 128]

    def flat_weights():
        return jnp.concatenate([wts[g] for g in range(GROUPS)], axis=1).astype(BF16)

    for load in loads[3:]:
        load.wait()
    for x in range(6):
        spread(feats[x], x + 1)
    for i in (1, 2):
        forward(i, flat_weights())
    start(2)
    start(4)

    for g in range(GROUPS):
        wtr[pl.ds(128 * g, 128), :] = jnp.concatenate([wts[g], wts[g]], axis=0).T
    half = lax.broadcasted_iota(jnp.int32, (32, 128), 1) < 64
    for ab in range(9):
        w0, w1, w2 = (wtr[pl.ds(32 * (3 * ab + e), 32), :] for e in range(3))
        even = jnp.where(half, w1, 0.0)
        odd = jnp.where(half, w2, w0)
        l_own[ab] = jnp.concatenate([even, odd], axis=0).astype(BF16)
    start(1)

    @pl.when(has_down)
    def _():
        arrived(0)
        spread(halo[...], 0)

    @pl.when(jnp.logical_not(has_down))
    def _():
        cells[0] = jnp.zeros(cells.shape[1:], BF16)

    forward(0, flat_weights())
    for i in (3, 5, 6):
        start(i)

    for i in (1, 2, 0):
        pre_grad = jnp.concatenate([pg_own[i, j] for j in range(3)], axis=1)
        part = matmul(pre_grad, patch(i), ((1,), (1,)))
        for g in range(GROUPS):
            piece = part[:, 128 * g : 128 * g + 128]
            grads[g] = piece if i == 1 else grads[g] + piece
    for g in range(GROUPS):
        rows = [grads[g, pl.ds(low, 16, stride=4), :] for low in range(4)]
        for tl in range(4):
            t = 4 * g + tl
            if t < TAPS:
                tile = jnp.zeros((16, 128), F32)
                for low in range(4):
                    turned = rows[low]
                    if tl != low:
                        turned = pltpu.roll(turned, ((low - tl) * 32) % 128, 1)
                    tile = jnp.where(chunk == low, turned, tile)
                tiles[t] = tile.astype(BF16)
    for t in range(TAPS, tiles.shape[0]):
        tiles[t] = jnp.zeros((16, 128), BF16)

    def near_copy(other, to):
        return pltpu.make_async_remote_copy(
            src_ref=tiles.at[pl.ds(other * share, share)], dst_ref=rs_got.at[me],
            send_sem=rs_send.at[other], recv_sem=rs_recv.at[me],
            device_id=to, device_id_type=MESH,
        )

    def near_arrival(other):
        return pltpu.make_async_remote_copy(
            src_ref=tiles.at[pl.ds(0, share)], dst_ref=rs_got.at[other],
            send_sem=rs_send.at[other], recv_sem=rs_recv.at[other],
            device_id=peer(1)[1], device_id_type=MESH,
        )

    def far_copy(other, to):
        return pltpu.make_async_remote_copy(
            src_ref=far_got.at[band], dst_ref=far_got.at[band],
            send_sem=far_send.at[other], recv_sem=far_recv.at[band],
            device_id=to, device_id_type=MESH,
        )

    def far_arrival(other):
        return pltpu.make_async_remote_copy(
            src_ref=far_got.at[other], dst_ref=far_got.at[other],
            send_sem=far_send.at[other], recv_sem=far_recv.at[other],
            device_id=far_peer(1)[1], device_id_type=MESH,
        )

    def ag_copy(other, to):
        return pltpu.make_async_remote_copy(
            src_ref=total, dst_ref=ag_got.at[pl.ds(me * share, share)],
            send_sem=ag_send.at[other], recv_sem=ag_recv.at[me],
            device_id=to, device_id_type=MESH,
        )

    def ag_arrival(other):
        return pltpu.make_async_remote_copy(
            src_ref=total, dst_ref=ag_got.at[pl.ds(other * share, share)],
            send_sem=ag_send.at[other], recv_sem=ag_recv.at[other],
            device_id=peer(1)[1], device_id_type=MESH,
        )

    def when_owner(who, action):
        @pl.when(who < owners)
        def _():
            action()

    for k in range(1, n_near):
        other, to = peer(k)
        when_owner(other, near_copy(other, to).start)

    def sum_near():
        rs_got[me] = tiles[pl.ds(me * share, share)]
        for k in range(1, n_near):
            near_arrival(peer(k)[0]).wait_recv()
        summed = rs_got[0].astype(F32)
        for k in range(1, n_near):
            summed += rs_got[k].astype(F32)
        far_got[band] = summed.astype(BF16)
        for k in range(1, n_far):
            far_copy(*far_peer(k)).start()

    inv_root = 1.0 / math.sqrt(n_dp * n_space * 3 * 3 * 128)

    def sum_far():
        for k in range(1, n_far):
            far_arrival(far_peer(k)[0]).wait_recv()
        summed = far_got[0].astype(F32)
        for k in range(1, n_far):
            summed += far_got[k].astype(F32)
        total[...] = (summed * inv_root).astype(BF16)
        for k in range(1, n_near):
            ag_copy(*peer(k)).start()
        ag_got[pl.ds(me * share, share)] = total[...]

    when_owner(me, sum_near)

    for i in (2, 3):
        arrived(i)

    @pl.when(has_prev)
    def _():
        act_out[...] = act_got[...]

    @pl.when(first_seg)
    def _():
        act_out[...] = jnp.zeros(act_out.shape, BF16)

    def planes(which, l_rows):
        put_r = lax.broadcasted_iota(jnp.int32, (256, 256), 0)
        put_c = lax.broadcasted_iota(jnp.int32, (256, 256), 1)
        weave = (put_c == 2 * (put_r % 128) + put_r // 128).astype(F32).astype(BF16)
        for i, pp in which:
            rows_i = [(1, i)] if pp == 0 else [(2, i), (0, i + 1)]
            lines = [None] * 6
            for qq in range(2):
                cols_j = [(1, 0)] if qq == 0 else [(2, 0), (0, 1)]
                left = jnp.concatenate(
                    [l_rows[3 * a + b] for a, _ in rows_i for b, _ in cols_j], axis=1
                )
                right = jnp.concatenate(
                    [
                        jnp.concatenate(
                            [shifted[ii, j + dj] for _, ii in rows_i for _, dj in cols_j], axis=0
                        )
                        for j in range(3)
                    ],
                    axis=1,
                )
                got = matmul(left, right).astype(BF16)
                for j in range(3):
                    line = got[:, 128 * j : 128 * j + 128]
                    lines[2 * j + qq] = jnp.concatenate([line[:32], line[32:]], axis=1)
            plane = matmul(jnp.concatenate(lines, axis=0), weave).astype(BF16)
            gin_out[2 * i + pp] = plane.reshape(6, 32, 256)

    inside = lax.broadcasted_iota(jnp.int32, (64, 128), 1) < 127

    def shift(i):
        for j in range(3):
            here = pg_got[i, j]
            moved = jnp.where(inside, pltpu.roll(here.astype(F32), 127, 1), 0.0)
            shifted[i, j, pl.ds(0, 64), :] = here
            shifted[i, j, pl.ds(64, 64), :] = moved.astype(BF16)
        shifted[i, 3] = jnp.zeros((128, 128), BF16)

    arrived(1)
    arrived(4)
    arrived(5)
    arrived(6)

    @pl.when(has_next)
    def _():
        @pl.when(jnp.logical_not(has_up))
        def _():
            pg_got[3] = jnp.zeros(pg_got.shape[1:], BF16)

        for i in range(4):
            shift(i)
        planes([(0, 0), (0, 1), (1, 0), (1, 1), (2, 0), (2, 1)], l_got)

    @pl.when(last_seg)
    def _():
        gin_out[...] = jnp.zeros(gin_out.shape, BF16)

    when_owner(me, sum_far)
    for k in range(1, n_near):
        other, _ = peer(k)
        when_owner(other, ag_arrival(other).wait_recv)
    for t in range(TAPS):
        rows = pl.ds(16 * t, 16)
        scaled = ag_got[t].astype(F32)
        prec_new = 0.75 * prec[rows] + 0.25 * scaled * scaled
        prec_out[rows] = prec_new
        mean_out[rows] = mean[rows] - 0.03 * scaled / (prec_new + 0.1)

    for i in range(len(links)):
        sent(i)

    for k in range(1, n_near):
        other, to = peer(k)
        when_owner(other, near_copy(other, to).wait_send)
        when_owner(me, ag_copy(other, to).wait_send)
    for k in range(1, n_far):
        when_owner(me, far_copy(*far_peer(k)).wait_send)


def deliver(*refs):
    done = refs[-1]
    copies = [pltpu.make_async_copy(refs[i], refs[4 + i], done.at[i]) for i in range(4)]
    for copy in copies:
        copy.start()
    for copy in copies:
        copy.wait()


def per_device(features, out_grad, weight_mean, weight_noise, precision):
    n_dp, n_seg, n_space = (lax.axis_size(a) for a in ("dp", "segment", "space"))
    near = 4 if n_space % 4 == 0 and n_space > 4 else 2
    n_near, n_far = n_dp * near, n_space // near
    share = -(-TAPS // n_near)
    feats = jnp.transpose(features[0, 0], (1, 2, 0, 3))
    og = jnp.transpose(out_grad[0, 0], (1, 2, 0, 3))
    mean, noise, prec = (
        w.reshape(TAPS * 16, 128) for w in (weight_mean, weight_noise, precision)
    )
    feats, og, mean, noise, prec = (
        pltpu.with_memory_space_constraint(v, pltpu.HBM) for v in (feats, og, mean, noise, prec)
    )
    vmem = pl.BlockSpec(memory_space=pltpu.VMEM)
    act, gin, mean_new, prec_new = pl.pallas_call(
        functools.partial(kernel, n_dp, n_seg, n_space, near, share),
        out_shape=[
            jax.ShapeDtypeStruct((3, 3, 64, 128), BF16),
            jax.ShapeDtypeStruct((6, 6, 32, 256), BF16),
            jax.ShapeDtypeStruct((TAPS * 16, 128), F32),
            jax.ShapeDtypeStruct((TAPS * 16, 128), F32),
        ],
        in_specs=[pl.BlockSpec(memory_space=pltpu.HBM)] * 5,
        out_specs=[vmem] * 4,
        scratch_shapes=[
            pltpu.VMEM((6, 6, 32, 256), BF16),
            pltpu.VMEM((3, 3, 64, 128), BF16),
            pltpu.VMEM((TAPS * 16, 128), F32),
            pltpu.VMEM((TAPS * 16, 128), F32),
            pltpu.VMEM((TAPS * 16, 128), F32),
            pltpu.VMEM((7, 7, 96, 128), BF16),
            pltpu.VMEM((GROUPS, 64, 128), F32),
            pltpu.VMEM((GROUPS * 128, 128), F32),
            pltpu.VMEM((9, 64, 128), BF16),
            pltpu.VMEM((9, 64, 128), BF16),
            pltpu.VMEM((6, 32, 256), BF16),
            pltpu.VMEM((3, 3, 64, 128), BF16),
            pltpu.VMEM((3, 3, 64, 128), BF16),
            pltpu.VMEM((3, 3, 64, 128), BF16),
            pltpu.VMEM((4, 3, 64, 128), BF16),
            pltpu.VMEM((4, 4, 128, 128), BF16),
            pltpu.VMEM((GROUPS, 64, 128), F32),
            pltpu.VMEM((n_near * share, 16, 128), BF16),
            pltpu.VMEM((n_near, share, 16, 128), BF16),
            pltpu.VMEM((n_far, share, 16, 128), BF16),
            pltpu.VMEM((share, 16, 128), BF16),
            pltpu.VMEM((n_near * share, 16, 128), BF16),
            pltpu.SemaphoreType.DMA((5,)),
            pltpu.SemaphoreType.DMA((7,)),
            pltpu.SemaphoreType.DMA((7,)),
            pltpu.SemaphoreType.DMA((n_near,)),
            pltpu.SemaphoreType.DMA((n_near,)),
            pltpu.SemaphoreType.DMA((n_far,)),
            pltpu.SemaphoreType.DMA((n_far,)),
            pltpu.SemaphoreType.DMA((n_near,)),
            pltpu.SemaphoreType.DMA((n_near,)),
        ],
        compiler_params=pltpu.CompilerParams(
            collective_id=0, has_side_effects=True, vmem_limit_bytes=40 * 2**20
        ),
        cost_estimate=pl.CostEstimate(
            flops=600_000_000, bytes_accessed=3_000_000, transcendentals=200_000
        ),
    )(feats, og, mean, noise, prec)
    act, gin, mean_new, prec_new = pl.pallas_call(
        deliver,
        out_shape=[jax.ShapeDtypeStruct(v.shape, v.dtype) for v in (act, gin, mean_new, prec_new)],
        in_specs=[vmem] * 4,
        out_specs=[pl.BlockSpec(memory_space=pltpu.HBM)] * 4,
        scratch_shapes=[pltpu.SemaphoreType.DMA((4,))],
        compiler_params=pltpu.CompilerParams(vmem_limit_bytes=2**20),
    )(act, gin, mean_new, prec_new)
    act = jnp.transpose(act, (2, 0, 1, 3))
    gin = jnp.transpose(gin, (2, 0, 1, 3))
    return (
        act[None, None],
        gin[None, None],
        mean_new.reshape(1, TAPS, 2048),
        prec_new.reshape(1, TAPS, 2048),
    )


def solution(mesh):
    in_specs = (
        P("dp", "segment", None, "space", None, None),
        P("dp", "segment", None, "space", None, None),
        P("segment", None, None),
        P("segment", None, None),
        P("segment", None, None),
    )
    out_specs = (
        P("dp", "segment", None, "space", None, None),
        P("dp", "segment", None, "space", None, None),
        P("segment", None, None),
        P("segment", None, None),
    )
    return jax.shard_map(
        per_device, mesh=mesh, in_specs=in_specs, out_specs=out_specs, check_vma=False
    )
```

```python
import functools
import math

import jax
import jax.numpy as jnp
from jax import lax
from jax.experimental import pallas as pl
from jax.experimental.pallas import tpu as pltpu
from jax.sharding import PartitionSpec as P

MESH = pl.DeviceIdType.MESH
BF16, F32 = jnp.bfloat16, jnp.float32
TAPS = 27
GROUPS = 7


def matmul(a, b, contract=((1,), (0,))):
    return lax.dot_general(a, b, (contract, ((), ())), preferred_element_type=F32)


def kernel(
    n_dp, n_seg, n_space, near, share,
    feats_hbm, og_hbm, mean_hbm, noise_hbm, prec_hbm,
    act_out, gin_out, mean_out, prec_out,
    feats, og, mean, noise, prec,
    cells, wts, wtr, l_own, l_got, halo, act_own, act_got, pg_own, pg_got, shifted,
    grads, tiles, rs_got, far_got, total, ag_got,
    heard, loaded, p_send, p_recv, rs_send, rs_recv, far_send, far_recv, ag_send, ag_recv,
):
    dp, seg, space = (lax.axis_index(a) for a in ("dp", "segment", "space"))
    n_near, n_far = n_dp * near, n_space // near
    owners = -(-TAPS // share)
    spot, band = lax.rem(space, near), space // near
    me = dp * near + spot
    first_seg, last_seg = seg == 0, seg == n_seg - 1
    has_next, has_prev = seg < n_seg - 1, seg > 0
    has_up, has_down = space < n_space - 1, space > 0

    def at(d, s, z):
        return {"dp": d, "segment": s, "space": z}

    def peer(k):
        other = lax.rem(me + k, n_near)
        return other, at(other // near, seg, band * near + lax.rem(other, near))

    def far_peer(k):
        other = lax.rem(band + k, n_far)
        return other, at(dp, seg, other * near + spot)

    def along(step):
        return lax.rem(space + step + n_space, n_space)

    barrier = pltpu.get_barrier_semaphore()
    steps = sorted({step % n_space for step in (-2, -1, 1, 2)})
    greeted = [(True, at(dp, seg, along(step))) for step in steps]
    for step in sorted({step % n_space for step in (-1, 0, 1)}):
        greeted += [(True, at(lax.rem(dp + k, n_dp), seg, along(step))) for k in range(1, n_dp)]
    greeted += [
        (has_prev, at(dp, seg - 1, space)),
        (has_next, at(dp, seg + 1, space)),
        (has_prev & has_down, at(dp, seg - 1, space - 1)),
        (has_next & has_up, at(dp, seg + 1, space + 1)),
    ]
    peers = 0
    for cond, to in greeted:
        if cond is True:
            pl.semaphore_signal(barrier, inc=1, device_id=to, device_id_type=MESH)
            peers = peers + 1
        else:
            @pl.when(cond)
            def _():
                pl.semaphore_signal(barrier, inc=1, device_id=to, device_id_type=MESH)

            peers = peers + cond.astype(jnp.int32)

    def tell(word, reach):
        for side, step in enumerate((reach, -reach)):
            pl.semaphore_signal(
                heard.at[word, side], inc=1, device_id=at(dp, seg, along(step)),
                device_id_type=MESH,
            )

    def hear(word):
        for side in range(2):
            pl.semaphore_wait(heard.at[word, side], 1)

    loads = [
        pltpu.make_async_copy(src, dst, loaded.at[i])
        for i, (src, dst) in enumerate(
            [(mean_hbm, mean), (noise_hbm, noise), (prec_hbm, prec), (feats_hbm, feats), (og_hbm, og)]
        )
    ]
    for load in loads:
        load.start()
    pl.semaphore_wait(barrier, peers)

    def link(i, src, dst, to):
        return pltpu.make_async_remote_copy(
            src_ref=src, dst_ref=dst, send_sem=p_send.at[i], recv_sem=p_recv.at[i],
            device_id=to, device_id_type=MESH,
        )

    prev = at(dp, seg - 1, space)
    after = at(dp, seg + 1, space)
    links = [
        (link(0, feats_hbm.at[feats_hbm.shape[0] - 1], halo, at(dp, seg, space + 1)), has_up, has_down),
        (link(1, l_own, l_got, prev), has_prev, has_next),
        (link(2, act_own.at[pl.ds(1, 2)], act_got.at[pl.ds(1, 2)], after), has_next, has_prev),
        (link(3, act_own.at[0], act_got.at[0], after), has_next, has_prev),
        (link(4, pg_own.at[pl.ds(1, 2)], pg_got.at[pl.ds(1, 2)], prev), has_prev, has_next),
        (link(5, pg_own.at[0], pg_got.at[0], prev), has_prev, has_next),
        (
            link(6, pg_own.at[0], pg_got.at[3], at(dp, seg - 1, space - 1)),
            has_prev & has_down,
            has_next & has_up,
        ),
    ]

    def start(i):
        copy, sends, _ = links[i]

        @pl.when(sends)
        def _():
            copy.start()

    def arrived(i):
        copy, _, receives = links[i]

        @pl.when(receives)
        def _():
            copy.wait_recv()

    def sent(i):
        copy, sends, _ = links[i]

        @pl.when(sends)
        def _():
            copy.wait_send()

    start(0)
    tell(0, 2)
    lane = lax.broadcasted_iota(jnp.int32, (16, 128), 1)
    chunk = lane // 32

    for load in loads[:3]:
        load.wait()
    slabs = []
    for t in range(TAPS):
        rows = pl.ds(16 * t, 16)
        slabs.append(mean[rows] + noise[rows] * lax.rsqrt(2000.0 * (prec[rows] + 0.1)))
    for g in range(GROUPS):
        for low in range(4):
            block = jnp.zeros((16, 128), F32)
            for tl in range(4):
                if 4 * g + tl < TAPS:
                    turned = slabs[4 * g + tl]
                    if tl != low:
                        turned = pltpu.roll(turned, ((tl - low) * 32) % 128, 1)
                    block = jnp.where(chunk == tl, turned, block)
            wts[g, pl.ds(low, 16, stride=4), :] = block

    z_of = lax.broadcasted_iota(jnp.int32, (256, 384), 0)
    column = lax.broadcasted_iota(jnp.int32, (256, 384), 1)
    pick = (z_of == 2 * (column % 128) + column // 128 - 1).astype(F32).astype(BF16)

    def spread(plane, x):
        got = matmul(plane.reshape(192, 256), pick).astype(BF16)
        for y in range(6):
            for e in range(3):
                cells[x, y + 1, pl.ds(32 * e, 32), :] = got[
                    32 * y : 32 * y + 32, 128 * e : 128 * e + 128
                ]

    for x in range(7):
        cells[x, 0] = jnp.zeros((96, 128), BF16)

    def patch(i):
        blocks = []
        for j in range(3):
            parts = [cells[2 * i + a, 2 * j : 2 * j + 3].reshape(288, 128) for a in range(3)]
            blocks.append(jnp.concatenate([*parts, jnp.zeros((32, 128), BF16)], axis=0))
        return jnp.concatenate(blocks, axis=1)

    def forward(i, weights):
        preact = matmul(weights, patch(i))
        grad = jnp.concatenate([og[i, j] for j in range(3)], axis=1).astype(F32)
        gate = jax.nn.sigmoid(preact)
        act = (preact * gate).astype(BF16)
        pre_grad = (grad * gate * (1.0 + preact * (1.0 - gate))).astype(BF16)
        for j in range(3):
            act_own[i, j] = act[:, 128 * j : 128 * j + 128]
            pg_own[i, j] = pre_grad[:, 128 * j : 128 * j + 128]

    def flat_weights():
        return jnp.concatenate([wts[g] for g in range(GROUPS)], axis=1).astype(BF16)

    for load in loads[3:]:
        load.wait()
    for x in range(6):
        spread(feats[x], x + 1)
    for i in (1, 2):
        forward(i, flat_weights())
    start(2)
    start(4)

    for g in range(GROUPS):
        wtr[pl.ds(128 * g, 128), :] = jnp.concatenate([wts[g], wts[g]], axis=0).T
    half = lax.broadcasted_iota(jnp.int32, (32, 128), 1) < 64
    for ab in range(9):
        w0, w1, w2 = (wtr[pl.ds(32 * (3 * ab + e), 32), :] for e in range(3))
        even = jnp.where(half, w1, 0.0)
        odd = jnp.where(half, w2, w0)
        l_own[ab] = jnp.concatenate([even, odd], axis=0).astype(BF16)
    start(1)

    @pl.when(has_down)
    def _():
        arrived(0)
        spread(halo[...], 0)

    @pl.when(jnp.logical_not(has_down))
    def _():
        cells[0] = jnp.zeros(cells.shape[1:], BF16)

    forward(0, flat_weights())
    hear(0)
    if n_space > 2 * near:
        tell(1, near)
    for i in (3, 5, 6):
        start(i)

    for i in (1, 2, 0):
        pre_grad = jnp.concatenate([pg_own[i, j] for j in range(3)], axis=1)
        part = matmul(pre_grad, patch(i), ((1,), (1,)))
        for g in range(GROUPS):
            piece = part[:, 128 * g : 128 * g + 128]
            grads[g] = piece if i == 1 else grads[g] + piece
    for g in range(GROUPS):
        rows = [grads[g, pl.ds(low, 16, stride=4), :] for low in range(4)]
        for tl in range(4):
            t = 4 * g + tl
            if t < TAPS:
                tile = jnp.zeros((16, 128), F32)
                for low in range(4):
                    turned = rows[low]
                    if tl != low:
                        turned = pltpu.roll(turned, ((low - tl) * 32) % 128, 1)
                    tile = jnp.where(chunk == low, turned, tile)
                tiles[t] = tile.astype(BF16)
    for t in range(TAPS, tiles.shape[0]):
        tiles[t] = jnp.zeros((16, 128), BF16)

    def near_copy(other, to):
        return pltpu.make_async_remote_copy(
            src_ref=tiles.at[pl.ds(other * share, share)], dst_ref=rs_got.at[me],
            send_sem=rs_send.at[other], recv_sem=rs_recv.at[me],
            device_id=to, device_id_type=MESH,
        )

    def near_arrival(other):
        return pltpu.make_async_remote_copy(
            src_ref=tiles.at[pl.ds(0, share)], dst_ref=rs_got.at[other],
            send_sem=rs_send.at[other], recv_sem=rs_recv.at[other],
            device_id=peer(1)[1], device_id_type=MESH,
        )

    def far_copy(other, to):
        return pltpu.make_async_remote_copy(
            src_ref=far_got.at[band], dst_ref=far_got.at[band],
            send_sem=far_send.at[other], recv_sem=far_recv.at[band],
            device_id=to, device_id_type=MESH,
        )

    def far_arrival(other):
        return pltpu.make_async_remote_copy(
            src_ref=far_got.at[other], dst_ref=far_got.at[other],
            send_sem=far_send.at[other], recv_sem=far_recv.at[other],
            device_id=far_peer(1)[1], device_id_type=MESH,
        )

    def ag_copy(other, to):
        return pltpu.make_async_remote_copy(
            src_ref=total, dst_ref=ag_got.at[pl.ds(me * share, share)],
            send_sem=ag_send.at[other], recv_sem=ag_recv.at[me],
            device_id=to, device_id_type=MESH,
        )

    def ag_arrival(other):
        return pltpu.make_async_remote_copy(
            src_ref=total, dst_ref=ag_got.at[pl.ds(other * share, share)],
            send_sem=ag_send.at[other], recv_sem=ag_recv.at[other],
            device_id=peer(1)[1], device_id_type=MESH,
        )

    def when_owner(who, action):
        @pl.when(who < owners)
        def _():
            action()

    for k in range(1, n_near):
        other, to = peer(k)
        when_owner(other, near_copy(other, to).start)

    def sum_near():
        rs_got[me] = tiles[pl.ds(me * share, share)]
        for k in range(1, n_near):
            near_arrival(peer(k)[0]).wait_recv()
        summed = rs_got[0].astype(F32)
        for k in range(1, n_near):
            summed += rs_got[k].astype(F32)
        far_got[band] = summed.astype(BF16)

    def go_far():
        for k in range(1, n_far):
            far_copy(*far_peer(k)).start()

    inv_root = 1.0 / math.sqrt(n_dp * n_space * 3 * 3 * 128)

    def sum_far():
        for k in range(1, n_far):
            far_arrival(far_peer(k)[0]).wait_recv()
        summed = far_got[0].astype(F32)
        for k in range(1, n_far):
            summed += far_got[k].astype(F32)
        total[...] = (summed * inv_root).astype(BF16)
        for k in range(1, n_near):
            ag_copy(*peer(k)).start()
        ag_got[pl.ds(me * share, share)] = total[...]

    when_owner(me, sum_near)
    if n_space > 2 * near:
        hear(1)
    when_owner(me, go_far)

    for i in (2, 3):
        arrived(i)

    @pl.when(has_prev)
    def _():
        act_out[...] = act_got[...]

    @pl.when(first_seg)
    def _():
        act_out[...] = jnp.zeros(act_out.shape, BF16)

    def planes(which, l_rows):
        put_r = lax.broadcasted_iota(jnp.int32, (256, 256), 0)
        put_c = lax.broadcasted_iota(jnp.int32, (256, 256), 1)
        weave = (put_c == 2 * (put_r % 128) + put_r // 128).astype(F32).astype(BF16)
        for i, pp in which:
            rows_i = [(1, i)] if pp == 0 else [(2, i), (0, i + 1)]
            lines = [None] * 6
            for qq in range(2):
                cols_j = [(1, 0)] if qq == 0 else [(2, 0), (0, 1)]
                left = jnp.concatenate(
                    [l_rows[3 * a + b] for a, _ in rows_i for b, _ in cols_j], axis=1
                )
                right = jnp.concatenate(
                    [
                        jnp.concatenate(
                            [shifted[ii, j + dj] for _, ii in rows_i for _, dj in cols_j], axis=0
                        )
                        for j in range(3)
                    ],
                    axis=1,
                )
                got = matmul(left, right).astype(BF16)
                for j in range(3):
                    line = got[:, 128 * j : 128 * j + 128]
                    lines[2 * j + qq] = jnp.concatenate([line[:32], line[32:]], axis=1)
            plane = matmul(jnp.concatenate(lines, axis=0), weave).astype(BF16)
            gin_out[2 * i + pp] = plane.reshape(6, 32, 256)

    inside = lax.broadcasted_iota(jnp.int32, (64, 128), 1) < 127

    def shift(i):
        for j in range(3):
            here = pg_got[i, j]
            moved = jnp.where(inside, pltpu.roll(here.astype(F32), 127, 1), 0.0)
            shifted[i, j, pl.ds(0, 64), :] = here
            shifted[i, j, pl.ds(64, 64), :] = moved.astype(BF16)
        shifted[i, 3] = jnp.zeros((128, 128), BF16)

    arrived(1)
    arrived(4)
    arrived(5)
    arrived(6)

    @pl.when(has_next)
    def _():
        @pl.when(jnp.logical_not(has_up))
        def _():
            pg_got[3] = jnp.zeros(pg_got.shape[1:], BF16)

        for i in range(4):
            shift(i)
        planes([(0, 0), (0, 1), (1, 0), (1, 1), (2, 0), (2, 1)], l_got)

    @pl.when(last_seg)
    def _():
        gin_out[...] = jnp.zeros(gin_out.shape, BF16)

    when_owner(me, sum_far)
    for k in range(1, n_near):
        other, _ = peer(k)
        when_owner(other, ag_arrival(other).wait_recv)
    for t in range(TAPS):
        rows = pl.ds(16 * t, 16)
        scaled = ag_got[t].astype(F32)
        prec_new = 0.75 * prec[rows] + 0.25 * scaled * scaled
        prec_out[rows] = prec_new
        mean_out[rows] = mean[rows] - 0.03 * scaled / (prec_new + 0.1)

    for i in range(len(links)):
        sent(i)

    for k in range(1, n_near):
        other, to = peer(k)
        when_owner(other, near_copy(other, to).wait_send)
        when_owner(me, ag_copy(other, to).wait_send)
    for k in range(1, n_far):
        when_owner(me, far_copy(*far_peer(k)).wait_send)


def deliver(*refs):
    done = refs[-1]
    copies = [pltpu.make_async_copy(refs[i], refs[4 + i], done.at[i]) for i in range(4)]
    for copy in copies:
        copy.start()
    for copy in copies:
        copy.wait()


def per_device(features, out_grad, weight_mean, weight_noise, precision):
    n_dp, n_seg, n_space = (lax.axis_size(a) for a in ("dp", "segment", "space"))
    near = 4 if n_space % 4 == 0 and n_space > 4 else 2
    n_near, n_far = n_dp * near, n_space // near
    share = -(-TAPS // n_near)
    feats = jnp.transpose(features[0, 0], (1, 2, 0, 3))
    og = jnp.transpose(out_grad[0, 0], (1, 2, 0, 3))
    mean, noise, prec = (
        w.reshape(TAPS * 16, 128) for w in (weight_mean, weight_noise, precision)
    )
    feats, og, mean, noise, prec = (
        pltpu.with_memory_space_constraint(v, pltpu.HBM) for v in (feats, og, mean, noise, prec)
    )
    vmem = pl.BlockSpec(memory_space=pltpu.VMEM)
    act, gin, mean_new, prec_new = pl.pallas_call(
        functools.partial(kernel, n_dp, n_seg, n_space, near, share),
        out_shape=[
            jax.ShapeDtypeStruct((3, 3, 64, 128), BF16),
            jax.ShapeDtypeStruct((6, 6, 32, 256), BF16),
            jax.ShapeDtypeStruct((TAPS * 16, 128), F32),
            jax.ShapeDtypeStruct((TAPS * 16, 128), F32),
        ],
        in_specs=[pl.BlockSpec(memory_space=pltpu.HBM)] * 5,
        out_specs=[vmem] * 4,
        scratch_shapes=[
            pltpu.VMEM((6, 6, 32, 256), BF16),
            pltpu.VMEM((3, 3, 64, 128), BF16),
            pltpu.VMEM((TAPS * 16, 128), F32),
            pltpu.VMEM((TAPS * 16, 128), F32),
            pltpu.VMEM((TAPS * 16, 128), F32),
            pltpu.VMEM((7, 7, 96, 128), BF16),
            pltpu.VMEM((GROUPS, 64, 128), F32),
            pltpu.VMEM((GROUPS * 128, 128), F32),
            pltpu.VMEM((9, 64, 128), BF16),
            pltpu.VMEM((9, 64, 128), BF16),
            pltpu.VMEM((6, 32, 256), BF16),
            pltpu.VMEM((3, 3, 64, 128), BF16),
            pltpu.VMEM((3, 3, 64, 128), BF16),
            pltpu.VMEM((3, 3, 64, 128), BF16),
            pltpu.VMEM((4, 3, 64, 128), BF16),
            pltpu.VMEM((4, 4, 128, 128), BF16),
            pltpu.VMEM((GROUPS, 64, 128), F32),
            pltpu.VMEM((n_near * share, 16, 128), BF16),
            pltpu.VMEM((n_near, share, 16, 128), BF16),
            pltpu.VMEM((n_far, share, 16, 128), BF16),
            pltpu.VMEM((share, 16, 128), BF16),
            pltpu.VMEM((n_near * share, 16, 128), BF16),
            pltpu.SemaphoreType.REGULAR((2, 2)),
            pltpu.SemaphoreType.DMA((5,)),
            pltpu.SemaphoreType.DMA((7,)),
            pltpu.SemaphoreType.DMA((7,)),
            pltpu.SemaphoreType.DMA((n_near,)),
            pltpu.SemaphoreType.DMA((n_near,)),
            pltpu.SemaphoreType.DMA((n_far,)),
            pltpu.SemaphoreType.DMA((n_far,)),
            pltpu.SemaphoreType.DMA((n_near,)),
            pltpu.SemaphoreType.DMA((n_near,)),
        ],
        compiler_params=pltpu.CompilerParams(
            collective_id=0, has_side_effects=True, vmem_limit_bytes=40 * 2**20
        ),
        cost_estimate=pl.CostEstimate(
            flops=600_000_000, bytes_accessed=3_000_000, transcendentals=200_000
        ),
    )(feats, og, mean, noise, prec)
    act, gin, mean_new, prec_new = pl.pallas_call(
        deliver,
        out_shape=[jax.ShapeDtypeStruct(v.shape, v.dtype) for v in (act, gin, mean_new, prec_new)],
        in_specs=[vmem] * 4,
        out_specs=[pl.BlockSpec(memory_space=pltpu.HBM)] * 4,
        scratch_shapes=[pltpu.SemaphoreType.DMA((4,))],
        compiler_params=pltpu.CompilerParams(vmem_limit_bytes=2**20),
    )(act, gin, mean_new, prec_new)
    act = jnp.transpose(act, (2, 0, 1, 3))
    gin = jnp.transpose(gin, (2, 0, 1, 3))
    return (
        act[None, None],
        gin[None, None],
        mean_new.reshape(1, TAPS, 2048),
        prec_new.reshape(1, TAPS, 2048),
    )


def solution(mesh):
    in_specs = (
        P("dp", "segment", None, "space", None, None),
        P("dp", "segment", None, "space", None, None),
        P("segment", None, None),
        P("segment", None, None),
        P("segment", None, None),
    )
    out_specs = (
        P("dp", "segment", None, "space", None, None),
        P("dp", "segment", None, "space", None, None),
        P("segment", None, None),
        P("segment", None, None),
    )
    return jax.shard_map(
        per_device, mesh=mesh, in_specs=in_specs, out_specs=out_specs, check_vma=False
    )
```

```python
import functools
import math

import jax
import jax.numpy as jnp
from jax import lax
from jax.experimental import pallas as pl
from jax.experimental.pallas import tpu as pltpu
from jax.sharding import PartitionSpec as P

MESH = pl.DeviceIdType.MESH
BF16, F32 = jnp.bfloat16, jnp.float32
TAPS = 27
GROUPS = 7


def matmul(a, b, contract=((1,), (0,))):
    return lax.dot_general(a, b, (contract, ((), ())), preferred_element_type=F32)


def kernel(
    n_dp, n_seg, n_space, near, share,
    feats_hbm, og_hbm, mean_hbm, noise_hbm, prec_hbm,
    act_out, gin_out, mean_out, prec_out,
    feats, og, mean, noise, prec,
    cells, wts, wtr, l_own, l_got, halo, act_own, act_got, pg_own, pg_got, shifted,
    grads, begun, tiles, rs_got, far_got, total, ag_got,
    heard, loaded, p_send, p_recv, rs_send, rs_recv, far_send, far_recv, ag_send, ag_recv,
):
    dp, seg, space = (lax.axis_index(a) for a in ("dp", "segment", "space"))
    n_near, n_far = n_dp * near, n_space // near
    owners = -(-TAPS // share)
    spot, band = lax.rem(space, near), space // near
    me = dp * near + spot
    odd = lax.rem(seg, 2)
    sums = (odd == 1) & (me < owners)
    mate = seg + 1 - 2 * odd
    first_seg, last_seg = seg == 0, seg == n_seg - 1
    has_next, has_prev = seg < n_seg - 1, seg > 0
    has_up, has_down = space < n_space - 1, space > 0

    def at(d, s, z):
        return {"dp": d, "segment": s, "space": z}

    def peer(k):
        other = lax.rem(me + k, n_near)
        return other, at(other // near, seg, band * near + lax.rem(other, near))

    def far_peer(k):
        other = lax.rem(band + k, n_far)
        return other, at(dp, seg, other * near + spot)

    def along(step):
        return lax.rem(space + step + n_space, n_space)

    barrier = pltpu.get_barrier_semaphore()
    greeted = []
    for which in (seg, mate):
        for step in sorted({step % n_space for step in (-2, -1, 1, 2)}):
            greeted.append((True, at(dp, which, along(step))))
        for step in sorted({step % n_space for step in (-1, 0, 1)}):
            for k in range(1, n_dp):
                greeted.append((True, at(lax.rem(dp + k, n_dp), which, along(step))))
    greeted += [
        (has_prev, at(dp, seg - 1, space)),
        (has_next, at(dp, seg + 1, space)),
        (has_prev & has_down, at(dp, seg - 1, space - 1)),
        (has_next & has_up, at(dp, seg + 1, space + 1)),
    ]
    peers = 0
    for cond, to in greeted:
        if cond is True:
            pl.semaphore_signal(barrier, inc=1, device_id=to, device_id_type=MESH)
            peers = peers + 1
        else:
            @pl.when(cond)
            def _():
                pl.semaphore_signal(barrier, inc=1, device_id=to, device_id_type=MESH)

            peers = peers + cond.astype(jnp.int32)

    def tell(word, reach):
        for side, step in enumerate((reach, -reach)):
            pl.semaphore_signal(
                heard.at[word, side], inc=1, device_id=at(dp, seg, along(step)),
                device_id_type=MESH,
            )

    def hear(word):
        for side in range(2):
            pl.semaphore_wait(heard.at[word, side], 1)

    loads = [
        pltpu.make_async_copy(src, dst, loaded.at[i])
        for i, (src, dst) in enumerate(
            [(mean_hbm, mean), (noise_hbm, noise), (prec_hbm, prec), (feats_hbm, feats), (og_hbm, og)]
        )
    ]
    for load in loads:
        load.start()
    pl.semaphore_wait(barrier, peers)

    def link(i, src, dst, to):
        return pltpu.make_async_remote_copy(
            src_ref=src, dst_ref=dst, send_sem=p_send.at[i], recv_sem=p_recv.at[i],
            device_id=to, device_id_type=MESH,
        )

    prev = at(dp, seg - 1, space)
    after = at(dp, seg + 1, space)
    links = [
        (link(0, feats_hbm.at[feats_hbm.shape[0] - 1], halo, at(dp, seg, space + 1)), has_up, has_down),
        (link(1, l_own, l_got, prev), has_prev, has_next),
        (link(2, act_own.at[pl.ds(1, 2)], act_got.at[pl.ds(1, 2)], after), has_next, has_prev),
        (link(3, act_own.at[0], act_got.at[0], after), has_next, has_prev),
        (link(4, pg_own.at[pl.ds(1, 2)], pg_got.at[pl.ds(1, 2)], prev), has_prev, has_next),
        (link(5, pg_own.at[0], pg_got.at[0], prev), has_prev, has_next),
        (
            link(6, pg_own.at[0], pg_got.at[3], at(dp, seg - 1, space - 1)),
            has_prev & has_down,
            has_next & has_up,
        ),
    ]

    def start(i):
        copy, sends, _ = links[i]

        @pl.when(sends)
        def _():
            copy.start()

    def arrived(i):
        copy, _, receives = links[i]

        @pl.when(receives)
        def _():
            copy.wait_recv()

    def sent(i):
        copy, sends, _ = links[i]

        @pl.when(sends)
        def _():
            copy.wait_send()

    start(0)
    tell(0, 2)
    lane = lax.broadcasted_iota(jnp.int32, (16, 128), 1)
    chunk = lane // 32

    for load in loads[:3]:
        load.wait()
    slabs = []
    for t in range(TAPS):
        rows = pl.ds(16 * t, 16)
        slabs.append(mean[rows] + noise[rows] * lax.rsqrt(2000.0 * (prec[rows] + 0.1)))
    for g in range(GROUPS):
        for low in range(4):
            block = jnp.zeros((16, 128), F32)
            for tl in range(4):
                if 4 * g + tl < TAPS:
                    turned = slabs[4 * g + tl]
                    if tl != low:
                        turned = pltpu.roll(turned, ((tl - low) * 32) % 128, 1)
                    block = jnp.where(chunk == tl, turned, block)
            wts[g, pl.ds(low, 16, stride=4), :] = block

    z_of = lax.broadcasted_iota(jnp.int32, (256, 384), 0)
    column = lax.broadcasted_iota(jnp.int32, (256, 384), 1)
    pick = (z_of == 2 * (column % 128) + column // 128 - 1).astype(F32).astype(BF16)

    def spread(plane, x):
        got = matmul(plane.reshape(192, 256), pick).astype(BF16)
        for y in range(6):
            for e in range(3):
                cells[x, y + 1, pl.ds(32 * e, 32), :] = got[
                    32 * y : 32 * y + 32, 128 * e : 128 * e + 128
                ]

    for x in range(7):
        cells[x, 0] = jnp.zeros((96, 128), BF16)

    def patch(i, low=0, high=3):
        columns = []
        for j in range(3):
            parts = [cells[2 * i + a, 2 * j : 2 * j + 3].reshape(288, 128) for a in range(low, high)]
            columns.append(jnp.concatenate(parts, axis=0))
        return jnp.concatenate(columns, axis=1)

    def finish(i, preact):
        grad = jnp.concatenate([og[i, j] for j in range(3)], axis=1).astype(F32)
        gate = jax.nn.sigmoid(preact)
        act = (preact * gate).astype(BF16)
        pre_grad = (grad * gate * (1.0 + preact * (1.0 - gate))).astype(BF16)
        for j in range(3):
            act_own[i, j] = act[:, 128 * j : 128 * j + 128]
            pg_own[i, j] = pre_grad[:, 128 * j : 128 * j + 128]

    def flat_weights():
        return jnp.concatenate([wts[g] for g in range(GROUPS)], axis=1)[:, : TAPS * 32].astype(BF16)

    for load in loads[3:]:
        load.wait()
    for x in range(6):
        spread(feats[x], x + 1)
    for i in (1, 2):
        finish(i, matmul(flat_weights(), patch(i)))
    start(2)
    start(4)

    for g in range(GROUPS):
        wtr[pl.ds(128 * g, 128), :] = jnp.concatenate([wts[g], wts[g]], axis=0).T
    half = lax.broadcasted_iota(jnp.int32, (32, 128), 1) < 64
    for ab in range(9):
        w0, w1, w2 = (wtr[pl.ds(32 * (3 * ab + e), 32), :] for e in range(3))
        even = jnp.where(half, w1, 0.0)
        skew = jnp.where(half, w2, w0)
        l_own[ab] = jnp.concatenate([even, skew], axis=0).astype(BF16)
    start(1)

    def grad_rows(i):
        return jnp.concatenate([pg_own[i, j] for j in range(3)], axis=1)

    for i in (1, 2):
        part = matmul(grad_rows(i), patch(i), ((1,), (1,)))
        for g in range(GROUPS):
            piece = part[:, 128 * g : 128 * g + 128]
            if g == GROUPS - 1:
                piece = jnp.concatenate([piece, jnp.zeros((64, 32), F32)], axis=1)
            grads[g] = piece if i == 1 else grads[g] + piece
    begun[...] = matmul(flat_weights()[:, 288:], patch(0, 1, 3))

    @pl.when(has_down)
    def _():
        arrived(0)
        spread(halo[...], 0)

    @pl.when(jnp.logical_not(has_down))
    def _():
        cells[0] = jnp.zeros(cells.shape[1:], BF16)

    finish(0, begun[...] + matmul(flat_weights()[:, :288], patch(0, 0, 1)))

    def near_copy(o):
        return pltpu.make_async_remote_copy(
            src_ref=tiles.at[pl.ds(o * share, share)], dst_ref=rs_got.at[odd, me],
            send_sem=rs_send.at[o], recv_sem=rs_recv.at[odd, me],
            device_id=at(o // near, seg + 1 - odd, band * near + o % near),
            device_id_type=MESH,
        )

    def near_arrival(pair, other):
        return pltpu.make_async_remote_copy(
            src_ref=tiles.at[pl.ds(0, share)], dst_ref=rs_got.at[pair, other],
            send_sem=rs_send.at[0], recv_sem=rs_recv.at[pair, other],
            device_id=peer(1)[1], device_id_type=MESH,
        )

    def far_copy(pair, k):
        other, to = far_peer(k)
        return pltpu.make_async_remote_copy(
            src_ref=far_got.at[pair, band], dst_ref=far_got.at[pair, band],
            send_sem=far_send.at[pair, other], recv_sem=far_recv.at[pair, band],
            device_id=to, device_id_type=MESH,
        )

    def far_arrival(pair, k):
        other, to = far_peer(k)
        return pltpu.make_async_remote_copy(
            src_ref=far_got.at[pair, other], dst_ref=far_got.at[pair, other],
            send_sem=far_send.at[pair, other], recv_sem=far_recv.at[pair, other],
            device_id=to, device_id_type=MESH,
        )

    def ag_copy(pair, k):
        other, _ = peer(k)
        return pltpu.make_async_remote_copy(
            src_ref=total.at[pair], dst_ref=ag_got.at[pl.ds(me * share, share)],
            send_sem=ag_send.at[pair, other], recv_sem=ag_recv.at[me],
            device_id=at(other // near, seg - 1 + pair, band * near + lax.rem(other, near)),
            device_id_type=MESH,
        )

    def ag_arrival(o):
        return pltpu.make_async_remote_copy(
            src_ref=total.at[0], dst_ref=ag_got.at[pl.ds(o * share, share)],
            send_sem=ag_send.at[0, 0], recv_sem=ag_recv.at[o],
            device_id=peer(1)[1], device_id_type=MESH,
        )

    last = matmul(grad_rows(0), patch(0), ((1,), (1,)))
    hear(0)
    if n_space > 2 * near:
        @pl.when(odd == 1)
        def _():
            tell(1, near)

    made = 0
    for g in range(GROUPS):
        piece = last[:, 128 * g : 128 * g + 128]
        if g == GROUPS - 1:
            piece = jnp.concatenate([piece, jnp.zeros((64, 32), F32)], axis=1)
        grads[g] = grads[g] + piece
        rows = [grads[g, pl.ds(low, 16, stride=4), :] for low in range(4)]
        for tl in range(4):
            t = 4 * g + tl
            if t < TAPS:
                tile = jnp.zeros((16, 128), F32)
                for low in range(4):
                    turned = rows[low]
                    if tl != low:
                        turned = pltpu.roll(turned, ((low - tl) * 32) % 128, 1)
                    tile = jnp.where(chunk == low, turned, tile)
                tiles[t] = tile.astype(BF16)
        if g == GROUPS - 1:
            for t in range(TAPS, tiles.shape[0]):
                tiles[t] = jnp.zeros((16, 128), BF16)
        while made < owners and ((made + 1) * share <= 4 * g + 4 or g == GROUPS - 1):
            @pl.when((me != made) | (odd == 0))
            def _(o=made):
                near_copy(o).start()

            made += 1
    for i in (5, 6, 3):
        start(i)

    inv_root = 1.0 / math.sqrt(n_dp * n_space * 3 * 3 * 128)

    def sum_near(pair):
        for k in range(pair, n_near):
            near_arrival(pair, peer(k)[0]).wait_recv()
        summed = rs_got[pair, 0].astype(F32)
        for k in range(1, n_near):
            summed += rs_got[pair, k].astype(F32)
        far_got[pair, band] = summed.astype(BF16)

    def go_far(pair):
        for k in range(1, n_far):
            far_copy(pair, k).start()

    def sum_far(pair):
        for k in range(1, n_far):
            far_arrival(pair, k).wait_recv()
        summed = far_got[pair, 0].astype(F32)
        for k in range(1, n_far):
            summed += far_got[pair, k].astype(F32)
        total[pair] = (summed * inv_root).astype(BF16)
        for k in range(pair, n_near):
            ag_copy(pair, k).start()

    @pl.when(sums)
    def _():
        rs_got[1, me] = tiles[pl.ds(me * share, share)]
        sum_near(1)

    if n_space > 2 * near:
        @pl.when(odd == 1)
        def _():
            hear(1)

    @pl.when(sums)
    def _():
        go_far(1)
        sum_near(0)
        go_far(0)

    for i in (2, 3):
        arrived(i)

    @pl.when(has_prev)
    def _():
        act_out[...] = act_got[...]

    @pl.when(first_seg)
    def _():
        act_out[...] = jnp.zeros(act_out.shape, BF16)

    def planes(which, l_rows):
        put_r = lax.broadcasted_iota(jnp.int32, (256, 256), 0)
        put_c = lax.broadcasted_iota(jnp.int32, (256, 256), 1)
        weave = (put_c == 2 * (put_r % 128) + put_r // 128).astype(F32).astype(BF16)
        for i, pp in which:
            rows_i = [(1, i)] if pp == 0 else [(2, i), (0, i + 1)]
            lines = [None] * 6
            for qq in range(2):
                cols_j = [(1, 0)] if qq == 0 else [(2, 0), (0, 1)]
                left = jnp.concatenate(
                    [l_rows[3 * a + b] for a, _ in rows_i for b, _ in cols_j], axis=1
                )
                right = jnp.concatenate(
                    [
                        jnp.concatenate(
                            [shifted[ii, j + dj] for _, ii in rows_i for _, dj in cols_j], axis=0
                        )
                        for j in range(3)
                    ],
                    axis=1,
                )
                got = matmul(left, right).astype(BF16)
                for j in range(3):
                    line = got[:, 128 * j : 128 * j + 128]
                    lines[2 * j + qq] = jnp.concatenate([line[:32], line[32:]], axis=1)
            plane = matmul(jnp.concatenate(lines, axis=0), weave).astype(BF16)
            gin_out[2 * i + pp] = plane.reshape(6, 32, 256)

    inside = lax.broadcasted_iota(jnp.int32, (64, 128), 1) < 127

    def shift(i):
        for j in range(3):
            here = pg_got[i, j]
            moved = jnp.where(inside, pltpu.roll(here.astype(F32), 127, 1), 0.0)
            shifted[i, j, pl.ds(0, 64), :] = here
            shifted[i, j, pl.ds(64, 64), :] = moved.astype(BF16)
        shifted[i, 3] = jnp.zeros((128, 128), BF16)

    arrived(1)
    arrived(4)
    arrived(5)
    arrived(6)

    @pl.when(has_next)
    def _():
        @pl.when(jnp.logical_not(has_up))
        def _():
            pg_got[3] = jnp.zeros(pg_got.shape[1:], BF16)

        for i in range(4):
            shift(i)
        planes([(0, 0), (0, 1), (1, 0), (1, 1), (2, 0), (2, 1)], l_got)

    @pl.when(last_seg)
    def _():
        gin_out[...] = jnp.zeros(gin_out.shape, BF16)

    @pl.when(sums)
    def _():
        sum_far(1)
        sum_far(0)
        ag_got[pl.ds(me * share, share)] = total[1]

    for t in range(TAPS):
        if t % share == 0:
            @pl.when((me != t // share) | (odd == 0))
            def _(o=t // share):
                ag_arrival(o).wait_recv()

        rows = pl.ds(16 * t, 16)
        scaled = ag_got[t].astype(F32)
        prec_new = 0.75 * prec[rows] + 0.25 * scaled * scaled
        prec_out[rows] = prec_new
        mean_out[rows] = mean[rows] - 0.03 * scaled / (prec_new + 0.1)

    for i in range(len(links)):
        sent(i)

    for o in range(owners):
        @pl.when((me != o) | (odd == 0))
        def _():
            near_copy(o).wait_send()

    @pl.when(sums)
    def _():
        for pair in range(2):
            for k in range(1, n_far):
                far_copy(pair, k).wait_send()
            for k in range(pair, n_near):
                ag_copy(pair, k).wait_send()


def deliver(*refs):
    done = refs[-1]
    parts = [(i, k) for i in (1, 0) for k in range(3)] + [(i, k) for i in (2, 3) for k in range(2)]
    copies = []
    for n, (i, k) in enumerate(parts):
        size = refs[i].shape[0] // (3 if i < 2 else 2)
        rows = pl.ds(size * k, size)
        copies.append(pltpu.make_async_copy(refs[i].at[rows], refs[4 + i].at[rows], done.at[n]))
    for copy in copies:
        copy.start()
    for copy in copies:
        copy.wait()


def per_device(features, out_grad, weight_mean, weight_noise, precision):
    n_dp, n_seg, n_space = (lax.axis_size(a) for a in ("dp", "segment", "space"))
    near = 4 if n_space % 4 == 0 and n_space > 4 else 2
    n_near, n_far = n_dp * near, n_space // near
    share = -(-TAPS // n_near)
    feats = jnp.transpose(features[0, 0], (1, 2, 0, 3))
    og = jnp.transpose(out_grad[0, 0], (1, 2, 0, 3))
    mean, noise, prec = (
        w.reshape(TAPS * 16, 128) for w in (weight_mean, weight_noise, precision)
    )
    feats, og, mean, noise, prec = (
        pltpu.with_memory_space_constraint(v, pltpu.HBM) for v in (feats, og, mean, noise, prec)
    )
    vmem = pl.BlockSpec(memory_space=pltpu.VMEM)
    act, gin, mean_new, prec_new = pl.pallas_call(
        functools.partial(kernel, n_dp, n_seg, n_space, near, share),
        out_shape=[
            jax.ShapeDtypeStruct((3, 3, 64, 128), BF16),
            jax.ShapeDtypeStruct((6, 6, 32, 256), BF16),
            jax.ShapeDtypeStruct((TAPS * 16, 128), F32),
            jax.ShapeDtypeStruct((TAPS * 16, 128), F32),
        ],
        in_specs=[pl.BlockSpec(memory_space=pltpu.HBM)] * 5,
        out_specs=[vmem] * 4,
        scratch_shapes=[
            pltpu.VMEM((6, 6, 32, 256), BF16),
            pltpu.VMEM((3, 3, 64, 128), BF16),
            pltpu.VMEM((TAPS * 16, 128), F32),
            pltpu.VMEM((TAPS * 16, 128), F32),
            pltpu.VMEM((TAPS * 16, 128), F32),
            pltpu.VMEM((7, 7, 96, 128), BF16),
            pltpu.VMEM((GROUPS, 64, 128), F32),
            pltpu.VMEM((GROUPS * 128, 128), F32),
            pltpu.VMEM((9, 64, 128), BF16),
            pltpu.VMEM((9, 64, 128), BF16),
            pltpu.VMEM((6, 32, 256), BF16),
            pltpu.VMEM((3, 3, 64, 128), BF16),
            pltpu.VMEM((3, 3, 64, 128), BF16),
            pltpu.VMEM((3, 3, 64, 128), BF16),
            pltpu.VMEM((4, 3, 64, 128), BF16),
            pltpu.VMEM((4, 4, 128, 128), BF16),
            pltpu.VMEM((GROUPS, 64, 128), F32),
            pltpu.VMEM((64, 384), F32),
            pltpu.VMEM((n_near * share, 16, 128), BF16),
            pltpu.VMEM((2, n_near, share, 16, 128), BF16),
            pltpu.VMEM((2, n_far, share, 16, 128), BF16),
            pltpu.VMEM((2, share, 16, 128), BF16),
            pltpu.VMEM((n_near * share, 16, 128), BF16),
            pltpu.SemaphoreType.REGULAR((2, 2)),
            pltpu.SemaphoreType.DMA((5,)),
            pltpu.SemaphoreType.DMA((7,)),
            pltpu.SemaphoreType.DMA((7,)),
            pltpu.SemaphoreType.DMA((n_near,)),
            pltpu.SemaphoreType.DMA((2, n_near)),
            pltpu.SemaphoreType.DMA((2, n_far)),
            pltpu.SemaphoreType.DMA((2, n_far)),
            pltpu.SemaphoreType.DMA((2, n_near)),
            pltpu.SemaphoreType.DMA((n_near,)),
        ],
        compiler_params=pltpu.CompilerParams(
            collective_id=0, has_side_effects=True, vmem_limit_bytes=40 * 2**20
        ),
        cost_estimate=pl.CostEstimate(
            flops=600_000_000, bytes_accessed=3_000_000, transcendentals=200_000
        ),
    )(feats, og, mean, noise, prec)
    act, gin, mean_new, prec_new = pl.pallas_call(
        deliver,
        out_shape=[jax.ShapeDtypeStruct(v.shape, v.dtype) for v in (act, gin, mean_new, prec_new)],
        in_specs=[vmem] * 4,
        out_specs=[pl.BlockSpec(memory_space=pltpu.HBM)] * 4,
        scratch_shapes=[pltpu.SemaphoreType.DMA((10,))],
        compiler_params=pltpu.CompilerParams(vmem_limit_bytes=2**20),
    )(act, gin, mean_new, prec_new)
    act = jnp.transpose(act, (2, 0, 1, 3))
    gin = jnp.transpose(gin, (2, 0, 1, 3))
    return (
        act[None, None],
        gin[None, None],
        mean_new.reshape(1, TAPS, 2048),
        prec_new.reshape(1, TAPS, 2048),
    )


def solution(mesh):
    in_specs = (
        P("dp", "segment", None, "space", None, None),
        P("dp", "segment", None, "space", None, None),
        P("segment", None, None),
        P("segment", None, None),
        P("segment", None, None),
    )
    out_specs = (
        P("dp", "segment", None, "space", None, None),
        P("dp", "segment", None, "space", None, None),
        P("segment", None, None),
        P("segment", None, None),
    )
    return jax.shard_map(
        per_device, mesh=mesh, in_specs=in_specs, out_specs=out_specs, check_vma=False
    )
```

```python
import functools
import math

import jax
import jax.numpy as jnp
from jax import lax
from jax.experimental import pallas as pl
from jax.experimental.pallas import tpu as pltpu
from jax.sharding import PartitionSpec as P

MESH = pl.DeviceIdType.MESH
BF16, F32 = jnp.bfloat16, jnp.float32
TAPS = 27
GROUPS = 7


def matmul(a, b, contract=((1,), (0,))):
    return lax.dot_general(a, b, (contract, ((), ())), preferred_element_type=F32)


def kernel(
    n_dp, n_seg, n_space, near, share,
    feats_hbm, og_hbm, mean_hbm, noise_hbm, prec_hbm,
    act_out, gin_out, mean_out, prec_out,
    feats, og, mean, noise, prec,
    cells, wts, wtr, l_own, l_got, halo, act_own, act_got, pg_own, pg_got, shifted,
    grads, begun, tiles, rs_got, far_got, total, ag_got,
    heard, loaded, p_send, p_recv, rs_send, rs_recv, far_send, far_recv, ag_send, ag_recv,
):
    dp, seg, space = (lax.axis_index(a) for a in ("dp", "segment", "space"))
    n_near, n_far = n_dp * near, n_space // near
    owners = -(-TAPS // share)
    spot, band = lax.rem(space, near), space // near
    me = dp * near + spot
    odd = lax.rem(seg, 2)
    sums = (odd == 1) & (me < owners)
    mate = seg + 1 - 2 * odd
    first_seg, last_seg = seg == 0, seg == n_seg - 1
    has_next, has_prev = seg < n_seg - 1, seg > 0
    has_up, has_down = space < n_space - 1, space > 0

    def at(d, s, z):
        return {"dp": d, "segment": s, "space": z}

    def peer(k):
        other = lax.rem(me + k, n_near)
        return other, at(other // near, seg, band * near + lax.rem(other, near))

    def far_peer(k):
        other = lax.rem(band + k, n_far)
        return other, at(dp, seg, other * near + spot)

    def along(step):
        return lax.rem(space + step + n_space, n_space)

    barrier = pltpu.get_barrier_semaphore()
    greeted = []
    for which in (seg, mate):
        for step in sorted({step % n_space for step in (-2, -1, 1, 2)}):
            greeted.append((True, at(dp, which, along(step))))
        for step in sorted({step % n_space for step in (-1, 0, 1)}):
            for k in range(1, n_dp):
                greeted.append((True, at(lax.rem(dp + k, n_dp), which, along(step))))
    greeted += [
        (has_prev, at(dp, seg - 1, space)),
        (has_next, at(dp, seg + 1, space)),
        (has_prev & has_down, at(dp, seg - 1, space - 1)),
        (has_next & has_up, at(dp, seg + 1, space + 1)),
    ]
    peers = 0
    for cond, to in greeted:
        if cond is True:
            pl.semaphore_signal(barrier, inc=1, device_id=to, device_id_type=MESH)
            peers = peers + 1
        else:
            @pl.when(cond)
            def _():
                pl.semaphore_signal(barrier, inc=1, device_id=to, device_id_type=MESH)

            peers = peers + cond.astype(jnp.int32)

    def tell(word, reach):
        for side, step in enumerate((reach, -reach)):
            pl.semaphore_signal(
                heard.at[word, side], inc=1, device_id=at(dp, seg, along(step)),
                device_id_type=MESH,
            )

    def hear(word):
        for side in range(2):
            pl.semaphore_wait(heard.at[word, side], 1)

    loads = [
        pltpu.make_async_copy(src, dst, loaded.at[i])
        for i, (src, dst) in enumerate(
            [(feats_hbm, feats), (mean_hbm, mean), (noise_hbm, noise), (prec_hbm, prec), (og_hbm, og)]
        )
    ]
    for load in loads:
        load.start()
    pl.semaphore_wait(barrier, peers)

    def link(i, src, dst, to):
        return pltpu.make_async_remote_copy(
            src_ref=src, dst_ref=dst, send_sem=p_send.at[i], recv_sem=p_recv.at[i],
            device_id=to, device_id_type=MESH,
        )

    prev = at(dp, seg - 1, space)
    after = at(dp, seg + 1, space)
    links = [
        (link(0, feats.at[feats.shape[0] - 1], halo, at(dp, seg, space + 1)), has_up, has_down),
        (link(1, l_own, l_got, prev), has_prev, has_next),
        (link(2, act_own.at[pl.ds(1, 2)], act_got.at[pl.ds(1, 2)], after), has_next, has_prev),
        (link(3, act_own.at[0], act_got.at[0], after), has_next, has_prev),
        (link(4, pg_own.at[pl.ds(1, 2)], pg_got.at[pl.ds(1, 2)], prev), has_prev, has_next),
        (link(5, pg_own.at[0], pg_got.at[0], prev), has_prev, has_next),
        (
            link(6, pg_own.at[0], pg_got.at[3], at(dp, seg - 1, space - 1)),
            has_prev & has_down,
            has_next & has_up,
        ),
    ]

    def start(i):
        copy, sends, _ = links[i]

        @pl.when(sends)
        def _():
            copy.start()

    def arrived(i):
        copy, _, receives = links[i]

        @pl.when(receives)
        def _():
            copy.wait_recv()

    def sent(i):
        copy, sends, _ = links[i]

        @pl.when(sends)
        def _():
            copy.wait_send()

    loads[0].wait()
    start(0)
    tell(0, 2)
    lane = lax.broadcasted_iota(jnp.int32, (16, 128), 1)
    chunk = lane // 32

    for load in loads[1:4]:
        load.wait()
    slabs = []
    for t in range(TAPS):
        rows = pl.ds(16 * t, 16)
        slabs.append(mean[rows] + noise[rows] * lax.rsqrt(2000.0 * (prec[rows] + 0.1)))
    for g in range(GROUPS):
        for low in range(4):
            block = jnp.zeros((16, 128), F32)
            for tl in range(4):
                if 4 * g + tl < TAPS:
                    turned = slabs[4 * g + tl]
                    if tl != low:
                        turned = pltpu.roll(turned, ((tl - low) * 32) % 128, 1)
                    block = jnp.where(chunk == tl, turned, block)
            wts[g, pl.ds(low, 16, stride=4), :] = block

    z_of = lax.broadcasted_iota(jnp.int32, (256, 384), 0)
    column = lax.broadcasted_iota(jnp.int32, (256, 384), 1)
    pick = (z_of == 2 * (column % 128) + column // 128 - 1).astype(F32).astype(BF16)

    def spread(plane, x):
        got = matmul(plane.reshape(192, 256), pick).astype(BF16)
        for y in range(6):
            for e in range(3):
                cells[x, y + 1, pl.ds(32 * e, 32), :] = got[
                    32 * y : 32 * y + 32, 128 * e : 128 * e + 128
                ]

    for x in range(7):
        cells[x, 0] = jnp.zeros((96, 128), BF16)

    def patch(i, low=0, high=3):
        columns = []
        for j in range(3):
            parts = [cells[2 * i + a, 2 * j : 2 * j + 3].reshape(288, 128) for a in range(low, high)]
            columns.append(jnp.concatenate(parts, axis=0))
        return jnp.concatenate(columns, axis=1)

    def finish(i, preact):
        grad = jnp.concatenate([og[i, j] for j in range(3)], axis=1).astype(F32)
        gate = jax.nn.sigmoid(preact)
        act = (preact * gate).astype(BF16)
        pre_grad = (grad * gate * (1.0 + preact * (1.0 - gate))).astype(BF16)
        for j in range(3):
            act_own[i, j] = act[:, 128 * j : 128 * j + 128]
            pg_own[i, j] = pre_grad[:, 128 * j : 128 * j + 128]

    def flat_weights():
        return jnp.concatenate([wts[g] for g in range(GROUPS)], axis=1)[:, : TAPS * 32].astype(BF16)

    loads[4].wait()
    for x in range(6):
        spread(feats[x], x + 1)
    for i in (1, 2):
        finish(i, matmul(flat_weights(), patch(i)))
    start(2)
    start(4)

    for g in range(GROUPS):
        wtr[pl.ds(128 * g, 128), :] = jnp.concatenate([wts[g], wts[g]], axis=0).T
    half = lax.broadcasted_iota(jnp.int32, (32, 128), 1) < 64
    for ab in range(9):
        w0, w1, w2 = (wtr[pl.ds(32 * (3 * ab + e), 32), :] for e in range(3))
        even = jnp.where(half, w1, 0.0)
        skew = jnp.where(half, w2, w0)
        l_own[ab] = jnp.concatenate([even, skew], axis=0).astype(BF16)
    start(1)

    def grad_rows(i):
        return jnp.concatenate([pg_own[i, j] for j in range(3)], axis=1)

    for i in (1, 2):
        part = matmul(grad_rows(i), patch(i), ((1,), (1,)))
        for g in range(GROUPS):
            piece = part[:, 128 * g : 128 * g + 128]
            if g == GROUPS - 1:
                piece = jnp.concatenate([piece, jnp.zeros((64, 32), F32)], axis=1)
            grads[g] = piece if i == 1 else grads[g] + piece
    begun[...] = matmul(flat_weights()[:, 288:], patch(0, 1, 3))

    @pl.when(has_down)
    def _():
        arrived(0)
        spread(halo[...], 0)

    @pl.when(jnp.logical_not(has_down))
    def _():
        cells[0] = jnp.zeros(cells.shape[1:], BF16)

    finish(0, begun[...] + matmul(flat_weights()[:, :288], patch(0, 0, 1)))

    def near_copy(o):
        return pltpu.make_async_remote_copy(
            src_ref=tiles.at[pl.ds(o * share, share)], dst_ref=rs_got.at[odd, me],
            send_sem=rs_send.at[o], recv_sem=rs_recv.at[odd, me],
            device_id=at(o // near, seg + 1 - odd, band * near + o % near),
            device_id_type=MESH,
        )

    def near_arrival(pair, other):
        return pltpu.make_async_remote_copy(
            src_ref=tiles.at[pl.ds(0, share)], dst_ref=rs_got.at[pair, other],
            send_sem=rs_send.at[0], recv_sem=rs_recv.at[pair, other],
            device_id=peer(1)[1], device_id_type=MESH,
        )

    def far_copy(pair, k):
        other, to = far_peer(k)
        return pltpu.make_async_remote_copy(
            src_ref=far_got.at[pair, band], dst_ref=far_got.at[pair, band],
            send_sem=far_send.at[pair, other], recv_sem=far_recv.at[pair, band],
            device_id=to, device_id_type=MESH,
        )

    def far_arrival(pair, k):
        other, to = far_peer(k)
        return pltpu.make_async_remote_copy(
            src_ref=far_got.at[pair, other], dst_ref=far_got.at[pair, other],
            send_sem=far_send.at[pair, other], recv_sem=far_recv.at[pair, other],
            device_id=to, device_id_type=MESH,
        )

    def ag_copy(pair, k):
        other, _ = peer(k)
        return pltpu.make_async_remote_copy(
            src_ref=total.at[pair], dst_ref=ag_got.at[pl.ds(me * share, share)],
            send_sem=ag_send.at[pair, other], recv_sem=ag_recv.at[me],
            device_id=at(other // near, seg - 1 + pair, band * near + lax.rem(other, near)),
            device_id_type=MESH,
        )

    def ag_arrival(o):
        return pltpu.make_async_remote_copy(
            src_ref=total.at[0], dst_ref=ag_got.at[pl.ds(o * share, share)],
            send_sem=ag_send.at[0, 0], recv_sem=ag_recv.at[o],
            device_id=peer(1)[1], device_id_type=MESH,
        )

    last = matmul(grad_rows(0), patch(0), ((1,), (1,)))
    hear(0)
    if n_space > 2 * near:
        @pl.when(odd == 1)
        def _():
            tell(1, near)

    made = 0
    for g in range(GROUPS):
        piece = last[:, 128 * g : 128 * g + 128]
        if g == GROUPS - 1:
            piece = jnp.concatenate([piece, jnp.zeros((64, 32), F32)], axis=1)
        grads[g] = grads[g] + piece
        rows = [grads[g, pl.ds(low, 16, stride=4), :] for low in range(4)]
        for tl in range(4):
            t = 4 * g + tl
            if t < TAPS:
                tile = jnp.zeros((16, 128), F32)
                for low in range(4):
                    turned = rows[low]
                    if tl != low:
                        turned = pltpu.roll(turned, ((low - tl) * 32) % 128, 1)
                    tile = jnp.where(chunk == low, turned, tile)
                tiles[t] = tile.astype(BF16)
        if g == GROUPS - 1:
            for t in range(TAPS, tiles.shape[0]):
                tiles[t] = jnp.zeros((16, 128), BF16)
        while made < owners and ((made + 1) * share <= 4 * g + 4 or g == GROUPS - 1):
            @pl.when((me != made) | (odd == 0))
            def _(o=made):
                near_copy(o).start()

            made += 1
    for i in (5, 6, 3):
        start(i)

    inv_root = 1.0 / math.sqrt(n_dp * n_space * 3 * 3 * 128)

    def sum_near(pair):
        for k in range(pair, n_near):
            near_arrival(pair, peer(k)[0]).wait_recv()
        summed = rs_got[pair, 0].astype(F32)
        for k in range(1, n_near):
            summed += rs_got[pair, k].astype(F32)
        far_got[pair, band] = summed.astype(BF16)

    def go_far(pair):
        for k in sorted(range(1, n_far), key=lambda k: -min(k, n_far - k)):
            far_copy(pair, k).start()

    def sum_far(pair):
        for k in range(1, n_far):
            far_arrival(pair, k).wait_recv()
        summed = far_got[pair, 0].astype(F32)
        for k in range(1, n_far):
            summed += far_got[pair, k].astype(F32)
        total[pair] = (summed * inv_root).astype(BF16)
        for k in range(pair, n_near):
            ag_copy(pair, k).start()

    @pl.when(sums)
    def _():
        rs_got[1, me] = tiles[pl.ds(me * share, share)]
        sum_near(1)

    if n_space > 2 * near:
        @pl.when(odd == 1)
        def _():
            hear(1)

    @pl.when(sums)
    def _():
        go_far(1)
        sum_near(0)
        go_far(0)

    for i in (2, 3):
        arrived(i)

    @pl.when(has_prev)
    def _():
        act_out[...] = act_got[...]

    @pl.when(first_seg)
    def _():
        act_out[...] = jnp.zeros(act_out.shape, BF16)

    def planes(which, l_rows):
        put_r = lax.broadcasted_iota(jnp.int32, (256, 256), 0)
        put_c = lax.broadcasted_iota(jnp.int32, (256, 256), 1)
        weave = (put_c == 2 * (put_r % 128) + put_r // 128).astype(F32).astype(BF16)
        for i, pp in which:
            rows_i = [(1, i)] if pp == 0 else [(2, i), (0, i + 1)]
            lines = [None] * 6
            for qq in range(2):
                cols_j = [(1, 0)] if qq == 0 else [(2, 0), (0, 1)]
                left = jnp.concatenate(
                    [l_rows[3 * a + b] for a, _ in rows_i for b, _ in cols_j], axis=1
                )
                right = jnp.concatenate(
                    [
                        jnp.concatenate(
                            [shifted[ii, j + dj] for _, ii in rows_i for _, dj in cols_j], axis=0
                        )
                        for j in range(3)
                    ],
                    axis=1,
                )
                got = matmul(left, right).astype(BF16)
                for j in range(3):
                    line = got[:, 128 * j : 128 * j + 128]
                    lines[2 * j + qq] = jnp.concatenate([line[:32], line[32:]], axis=1)
            plane = matmul(jnp.concatenate(lines, axis=0), weave).astype(BF16)
            gin_out[2 * i + pp] = plane.reshape(6, 32, 256)

    inside = lax.broadcasted_iota(jnp.int32, (64, 128), 1) < 127

    def shift(i):
        for j in range(3):
            here = pg_got[i, j]
            moved = jnp.where(inside, pltpu.roll(here.astype(F32), 127, 1), 0.0)
            shifted[i, j, pl.ds(0, 64), :] = here
            shifted[i, j, pl.ds(64, 64), :] = moved.astype(BF16)
        shifted[i, 3] = jnp.zeros((128, 128), BF16)

    arrived(1)
    arrived(4)
    arrived(5)
    arrived(6)

    @pl.when(has_next)
    def _():
        @pl.when(jnp.logical_not(has_up))
        def _():
            pg_got[3] = jnp.zeros(pg_got.shape[1:], BF16)

        for i in range(4):
            shift(i)
        planes([(0, 0), (0, 1), (1, 0), (1, 1), (2, 0), (2, 1)], l_got)

    @pl.when(last_seg)
    def _():
        gin_out[...] = jnp.zeros(gin_out.shape, BF16)

    @pl.when(sums)
    def _():
        sum_far(1)
        sum_far(0)
        ag_got[pl.ds(me * share, share)] = total[1]

    for t in range(TAPS):
        if t % share == 0:
            @pl.when((me != t // share) | (odd == 0))
            def _(o=t // share):
                ag_arrival(o).wait_recv()

        rows = pl.ds(16 * t, 16)
        scaled = ag_got[t].astype(F32)
        prec_new = 0.75 * prec[rows] + 0.25 * scaled * scaled
        prec_out[rows] = prec_new
        mean_out[rows] = mean[rows] - 0.03 * scaled / (prec_new + 0.1)

    for i in range(len(links)):
        sent(i)

    for o in range(owners):
        @pl.when((me != o) | (odd == 0))
        def _():
            near_copy(o).wait_send()

    @pl.when(sums)
    def _():
        for pair in range(2):
            for k in range(1, n_far):
                far_copy(pair, k).wait_send()
            for k in range(pair, n_near):
                ag_copy(pair, k).wait_send()


def deliver(*refs):
    done = refs[-1]
    parts = [(i, k) for i in (1, 0) for k in range(3)] + [(i, k) for i in (2, 3) for k in range(2)]
    copies = []
    for n, (i, k) in enumerate(parts):
        size = refs[i].shape[0] // (3 if i < 2 else 2)
        rows = pl.ds(size * k, size)
        copies.append(pltpu.make_async_copy(refs[i].at[rows], refs[4 + i].at[rows], done.at[n]))
    for copy in copies:
        copy.start()
    for copy in copies:
        copy.wait()


def per_device(features, out_grad, weight_mean, weight_noise, precision):
    n_dp, n_seg, n_space = (lax.axis_size(a) for a in ("dp", "segment", "space"))
    near = 4 if n_space % 4 == 0 and n_space > 4 else 2
    n_near, n_far = n_dp * near, n_space // near
    share = -(-TAPS // n_near)
    feats = jnp.transpose(features[0, 0], (1, 2, 0, 3))
    og = jnp.transpose(out_grad[0, 0], (1, 2, 0, 3))
    mean, noise, prec = (
        w.reshape(TAPS * 16, 128) for w in (weight_mean, weight_noise, precision)
    )
    feats, og, mean, noise, prec = (
        pltpu.with_memory_space_constraint(v, pltpu.HBM) for v in (feats, og, mean, noise, prec)
    )
    vmem = pl.BlockSpec(memory_space=pltpu.VMEM)
    act, gin, mean_new, prec_new = pl.pallas_call(
        functools.partial(kernel, n_dp, n_seg, n_space, near, share),
        out_shape=[
            jax.ShapeDtypeStruct((3, 3, 64, 128), BF16),
            jax.ShapeDtypeStruct((6, 6, 32, 256), BF16),
            jax.ShapeDtypeStruct((TAPS * 16, 128), F32),
            jax.ShapeDtypeStruct((TAPS * 16, 128), F32),
        ],
        in_specs=[pl.BlockSpec(memory_space=pltpu.HBM)] * 5,
        out_specs=[vmem] * 4,
        scratch_shapes=[
            pltpu.VMEM((6, 6, 32, 256), BF16),
            pltpu.VMEM((3, 3, 64, 128), BF16),
            pltpu.VMEM((TAPS * 16, 128), F32),
            pltpu.VMEM((TAPS * 16, 128), F32),
            pltpu.VMEM((TAPS * 16, 128), F32),
            pltpu.VMEM((7, 7, 96, 128), BF16),
            pltpu.VMEM((GROUPS, 64, 128), F32),
            pltpu.VMEM((GROUPS * 128, 128), F32),
            pltpu.VMEM((9, 64, 128), BF16),
            pltpu.VMEM((9, 64, 128), BF16),
            pltpu.VMEM((6, 32, 256), BF16),
            pltpu.VMEM((3, 3, 64, 128), BF16),
            pltpu.VMEM((3, 3, 64, 128), BF16),
            pltpu.VMEM((3, 3, 64, 128), BF16),
            pltpu.VMEM((4, 3, 64, 128), BF16),
            pltpu.VMEM((4, 4, 128, 128), BF16),
            pltpu.VMEM((GROUPS, 64, 128), F32),
            pltpu.VMEM((64, 384), F32),
            pltpu.VMEM((n_near * share, 16, 128), BF16),
            pltpu.VMEM((2, n_near, share, 16, 128), BF16),
            pltpu.VMEM((2, n_far, share, 16, 128), BF16),
            pltpu.VMEM((2, share, 16, 128), BF16),
            pltpu.VMEM((n_near * share, 16, 128), BF16),
            pltpu.SemaphoreType.REGULAR((2, 2)),
            pltpu.SemaphoreType.DMA((5,)),
            pltpu.SemaphoreType.DMA((7,)),
            pltpu.SemaphoreType.DMA((7,)),
            pltpu.SemaphoreType.DMA((n_near,)),
            pltpu.SemaphoreType.DMA((2, n_near)),
            pltpu.SemaphoreType.DMA((2, n_far)),
            pltpu.SemaphoreType.DMA((2, n_far)),
            pltpu.SemaphoreType.DMA((2, n_near)),
            pltpu.SemaphoreType.DMA((n_near,)),
        ],
        compiler_params=pltpu.CompilerParams(
            collective_id=0, has_side_effects=True, vmem_limit_bytes=40 * 2**20
        ),
        cost_estimate=pl.CostEstimate(
            flops=600_000_000, bytes_accessed=3_000_000, transcendentals=200_000
        ),
    )(feats, og, mean, noise, prec)
    act, gin, mean_new, prec_new = pl.pallas_call(
        deliver,
        out_shape=[jax.ShapeDtypeStruct(v.shape, v.dtype) for v in (act, gin, mean_new, prec_new)],
        in_specs=[vmem] * 4,
        out_specs=[pl.BlockSpec(memory_space=pltpu.HBM)] * 4,
        scratch_shapes=[pltpu.SemaphoreType.DMA((10,))],
        compiler_params=pltpu.CompilerParams(vmem_limit_bytes=2**20),
    )(act, gin, mean_new, prec_new)
    act = jnp.transpose(act, (2, 0, 1, 3))
    gin = jnp.transpose(gin, (2, 0, 1, 3))
    return (
        act[None, None],
        gin[None, None],
        mean_new.reshape(1, TAPS, 2048),
        prec_new.reshape(1, TAPS, 2048),
    )


def solution(mesh):
    in_specs = (
        P("dp", "segment", None, "space", None, None),
        P("dp", "segment", None, "space", None, None),
        P("segment", None, None),
        P("segment", None, None),
        P("segment", None, None),
    )
    out_specs = (
        P("dp", "segment", None, "space", None, None),
        P("dp", "segment", None, "space", None, None),
        P("segment", None, None),
        P("segment", None, None),
    )
    return jax.shard_map(
        per_device, mesh=mesh, in_specs=in_specs, out_specs=out_specs, check_vma=False
    )
```

```python
import functools
import math

import jax
import jax.numpy as jnp
from jax import lax
from jax.experimental import pallas as pl
from jax.experimental.pallas import tpu as pltpu
from jax.sharding import PartitionSpec as P

MESH = pl.DeviceIdType.MESH
BF16, F32 = jnp.bfloat16, jnp.float32
TAPS = 27
GROUPS = 7


def matmul(a, b, contract=((1,), (0,))):
    return lax.dot_general(a, b, (contract, ((), ())), preferred_element_type=F32)


def kernel(
    n_dp, n_seg, n_space, near, share,
    feats_hbm, og_hbm, mean_hbm, noise_hbm, prec_hbm,
    act_out, gin_out, mean_out, prec_out, scaled_out,
    feats, og, mean, noise, prec,
    cells, wts, wtr, l_own, l_got, halo, act_own, act_got, pg_own, pg_got, shifted,
    grads, begun, tiles, rs_got, far_got, total, ag_got,
    heard, loaded, p_send, p_recv, rs_send, rs_recv, far_send, far_recv, ag_send, ag_recv,
):
    dp, seg, space = (lax.axis_index(a) for a in ("dp", "segment", "space"))
    n_near, n_far = n_dp * near, n_space // near
    owners = -(-TAPS // share)
    spot, band = lax.rem(space, near), space // near
    me = dp * near + spot
    odd = lax.rem(seg, 2)
    sums = (odd == 1) & (me < owners)
    mate = seg + 1 - 2 * odd
    first_seg, last_seg = seg == 0, seg == n_seg - 1
    has_next, has_prev = seg < n_seg - 1, seg > 0
    has_up, has_down = space < n_space - 1, space > 0

    def at(d, s, z):
        return {"dp": d, "segment": s, "space": z}

    def peer(k):
        other = lax.rem(me + k, n_near)
        return other, at(other // near, seg, band * near + lax.rem(other, near))

    def far_peer(k):
        other = lax.rem(band + k, n_far)
        return other, at(dp, seg, other * near + spot)

    def along(step):
        return lax.rem(space + step + n_space, n_space)

    barrier = pltpu.get_barrier_semaphore()
    greeted = []
    for which in (seg, mate):
        for step in sorted({step % n_space for step in (-2, -1, 1, 2)}):
            greeted.append((True, at(dp, which, along(step))))
        for step in sorted({step % n_space for step in (-1, 0, 1)}):
            for k in range(1, n_dp):
                greeted.append((True, at(lax.rem(dp + k, n_dp), which, along(step))))
    greeted += [
        (has_prev, at(dp, seg - 1, space)),
        (has_next, at(dp, seg + 1, space)),
        (has_prev & has_down, at(dp, seg - 1, space - 1)),
        (has_next & has_up, at(dp, seg + 1, space + 1)),
    ]
    peers = 0
    for cond, to in greeted:
        if cond is True:
            pl.semaphore_signal(barrier, inc=1, device_id=to, device_id_type=MESH)
            peers = peers + 1
        else:
            @pl.when(cond)
            def _():
                pl.semaphore_signal(barrier, inc=1, device_id=to, device_id_type=MESH)

            peers = peers + cond.astype(jnp.int32)

    def tell(word, reach):
        for side, step in enumerate((reach, -reach)):
            pl.semaphore_signal(
                heard.at[word, side], inc=1, device_id=at(dp, seg, along(step)),
                device_id_type=MESH,
            )

    def hear(word):
        for side in range(2):
            pl.semaphore_wait(heard.at[word, side], 1)

    loads = [
        pltpu.make_async_copy(src, dst, loaded.at[i])
        for i, (src, dst) in enumerate(
            [(feats_hbm, feats), (mean_hbm, mean), (noise_hbm, noise), (prec_hbm, prec), (og_hbm, og)]
        )
    ]
    for load in loads:
        load.start()
    pl.semaphore_wait(barrier, peers)

    def link(i, src, dst, to):
        return pltpu.make_async_remote_copy(
            src_ref=src, dst_ref=dst, send_sem=p_send.at[i], recv_sem=p_recv.at[i],
            device_id=to, device_id_type=MESH,
        )

    prev = at(dp, seg - 1, space)
    after = at(dp, seg + 1, space)
    links = [
        (link(0, feats.at[feats.shape[0] - 1], halo, at(dp, seg, space + 1)), has_up, has_down),
        (link(1, l_own, l_got, prev), has_prev, has_next),
        (link(2, act_own.at[pl.ds(1, 2)], act_got.at[pl.ds(1, 2)], after), has_next, has_prev),
        (link(3, act_own.at[0], act_got.at[0], after), has_next, has_prev),
        (link(4, pg_own.at[pl.ds(1, 2)], pg_got.at[pl.ds(1, 2)], prev), has_prev, has_next),
        (link(5, pg_own.at[0], pg_got.at[0], prev), has_prev, has_next),
        (
            link(6, pg_own.at[0], pg_got.at[3], at(dp, seg - 1, space - 1)),
            has_prev & has_down,
            has_next & has_up,
        ),
    ]

    def start(i):
        copy, sends, _ = links[i]

        @pl.when(sends)
        def _():
            copy.start()

    def arrived(i):
        copy, _, receives = links[i]

        @pl.when(receives)
        def _():
            copy.wait_recv()

    def sent(i):
        copy, sends, _ = links[i]

        @pl.when(sends)
        def _():
            copy.wait_send()

    loads[0].wait()
    start(0)
    tell(0, 2)
    lane = lax.broadcasted_iota(jnp.int32, (16, 128), 1)
    chunk = lane // 32

    for load in loads[1:4]:
        load.wait()
    slabs = []
    for t in range(TAPS):
        rows = pl.ds(16 * t, 16)
        slabs.append(mean[rows] + noise[rows] * lax.rsqrt(2000.0 * (prec[rows] + 0.1)))
    for g in range(GROUPS):
        for low in range(4):
            block = jnp.zeros((16, 128), F32)
            for tl in range(4):
                if 4 * g + tl < TAPS:
                    turned = slabs[4 * g + tl]
                    if tl != low:
                        turned = pltpu.roll(turned, ((tl - low) * 32) % 128, 1)
                    block = jnp.where(chunk == tl, turned, block)
            wts[g, pl.ds(low, 16, stride=4), :] = block

    z_of = lax.broadcasted_iota(jnp.int32, (256, 384), 0)
    column = lax.broadcasted_iota(jnp.int32, (256, 384), 1)
    pick = (z_of == 2 * (column % 128) + column // 128 - 1).astype(F32).astype(BF16)

    def spread(plane, x):
        got = matmul(plane.reshape(192, 256), pick).astype(BF16)
        for y in range(6):
            for e in range(3):
                cells[x, y + 1, pl.ds(32 * e, 32), :] = got[
                    32 * y : 32 * y + 32, 128 * e : 128 * e + 128
                ]

    for x in range(7):
        cells[x, 0] = jnp.zeros((96, 128), BF16)

    def patch(i, low=0, high=3):
        columns = []
        for j in range(3):
            parts = [cells[2 * i + a, 2 * j : 2 * j + 3].reshape(288, 128) for a in range(low, high)]
            columns.append(jnp.concatenate(parts, axis=0))
        return jnp.concatenate(columns, axis=1)

    def finish(i, preact):
        grad = jnp.concatenate([og[i, j] for j in range(3)], axis=1).astype(F32)
        gate = jax.nn.sigmoid(preact)
        act = (preact * gate).astype(BF16)
        pre_grad = (grad * gate * (1.0 + preact * (1.0 - gate))).astype(BF16)
        for j in range(3):
            act_own[i, j] = act[:, 128 * j : 128 * j + 128]
            pg_own[i, j] = pre_grad[:, 128 * j : 128 * j + 128]

    def flat_weights():
        return jnp.concatenate([wts[g] for g in range(GROUPS)], axis=1)[:, : TAPS * 32].astype(BF16)

    loads[4].wait()
    for x in range(6):
        spread(feats[x], x + 1)
    for i in (1, 2):
        finish(i, matmul(flat_weights(), patch(i)))
    start(2)
    start(4)

    for g in range(GROUPS):
        wtr[pl.ds(128 * g, 128), :] = jnp.concatenate([wts[g], wts[g]], axis=0).T
    half = lax.broadcasted_iota(jnp.int32, (32, 128), 1) < 64
    for ab in range(9):
        w0, w1, w2 = (wtr[pl.ds(32 * (3 * ab + e), 32), :] for e in range(3))
        even = jnp.where(half, w1, 0.0)
        skew = jnp.where(half, w2, w0)
        l_own[ab] = jnp.concatenate([even, skew], axis=0).astype(BF16)
    start(1)

    def grad_rows(i):
        return jnp.concatenate([pg_own[i, j] for j in range(3)], axis=1)

    for i in (1, 2):
        part = matmul(grad_rows(i), patch(i), ((1,), (1,)))
        for g in range(GROUPS):
            piece = part[:, 128 * g : 128 * g + 128]
            if g == GROUPS - 1:
                piece = jnp.concatenate([piece, jnp.zeros((64, 32), F32)], axis=1)
            grads[g] = piece if i == 1 else grads[g] + piece
    begun[...] = matmul(flat_weights()[:, 288:], patch(0, 1, 3))

    @pl.when(has_down)
    def _():
        arrived(0)
        spread(halo[...], 0)

    @pl.when(jnp.logical_not(has_down))
    def _():
        cells[0] = jnp.zeros(cells.shape[1:], BF16)

    finish(0, begun[...] + matmul(flat_weights()[:, :288], patch(0, 0, 1)))

    def near_copy(o):
        return pltpu.make_async_remote_copy(
            src_ref=tiles.at[pl.ds(o * share, share)], dst_ref=rs_got.at[odd, me],
            send_sem=rs_send.at[o], recv_sem=rs_recv.at[odd, me],
            device_id=at(o // near, seg + 1 - odd, band * near + o % near),
            device_id_type=MESH,
        )

    def near_arrival(pair, other):
        return pltpu.make_async_remote_copy(
            src_ref=tiles.at[pl.ds(0, share)], dst_ref=rs_got.at[pair, other],
            send_sem=rs_send.at[0], recv_sem=rs_recv.at[pair, other],
            device_id=peer(1)[1], device_id_type=MESH,
        )

    def far_copy(pair, k):
        other, to = far_peer(k)
        return pltpu.make_async_remote_copy(
            src_ref=far_got.at[pair, band], dst_ref=far_got.at[pair, band],
            send_sem=far_send.at[pair, other], recv_sem=far_recv.at[pair, band],
            device_id=to, device_id_type=MESH,
        )

    def far_arrival(pair, k):
        other, to = far_peer(k)
        return pltpu.make_async_remote_copy(
            src_ref=far_got.at[pair, other], dst_ref=far_got.at[pair, other],
            send_sem=far_send.at[pair, other], recv_sem=far_recv.at[pair, other],
            device_id=to, device_id_type=MESH,
        )

    def ag_copy(pair, k):
        other, _ = peer(k)
        return pltpu.make_async_remote_copy(
            src_ref=total.at[pair], dst_ref=ag_got.at[pl.ds(me * share, share)],
            send_sem=ag_send.at[pair, other], recv_sem=ag_recv.at[me],
            device_id=at(other // near, seg - 1 + pair, band * near + lax.rem(other, near)),
            device_id_type=MESH,
        )

    def ag_arrival(o):
        return pltpu.make_async_remote_copy(
            src_ref=total.at[0], dst_ref=ag_got.at[pl.ds(o * share, share)],
            send_sem=ag_send.at[0, 0], recv_sem=ag_recv.at[o],
            device_id=peer(1)[1], device_id_type=MESH,
        )

    last = matmul(grad_rows(0), patch(0), ((1,), (1,)))
    hear(0)
    if n_space > 2 * near:
        @pl.when(odd == 1)
        def _():
            tell(1, near)

    made = 0
    for g in range(GROUPS):
        piece = last[:, 128 * g : 128 * g + 128]
        if g == GROUPS - 1:
            piece = jnp.concatenate([piece, jnp.zeros((64, 32), F32)], axis=1)
        grads[g] = grads[g] + piece
        rows = [grads[g, pl.ds(low, 16, stride=4), :] for low in range(4)]
        for tl in range(4):
            t = 4 * g + tl
            if t < TAPS:
                tile = jnp.zeros((16, 128), F32)
                for low in range(4):
                    turned = rows[low]
                    if tl != low:
                        turned = pltpu.roll(turned, ((low - tl) * 32) % 128, 1)
                    tile = jnp.where(chunk == low, turned, tile)
                tiles[t] = tile.astype(BF16)
        if g == GROUPS - 1:
            for t in range(TAPS, tiles.shape[0]):
                tiles[t] = jnp.zeros((16, 128), BF16)
        while made < owners and ((made + 1) * share <= 4 * g + 4 or g == GROUPS - 1):
            @pl.when((me != made) | (odd == 0))
            def _(o=made):
                near_copy(o).start()

            made += 1
    for i in (5, 6, 3):
        start(i)

    inv_root = 1.0 / math.sqrt(n_dp * n_space * 3 * 3 * 128)

    def sum_near(pair):
        for k in range(pair, n_near):
            near_arrival(pair, peer(k)[0]).wait_recv()
        summed = rs_got[pair, 0].astype(F32)
        for k in range(1, n_near):
            summed += rs_got[pair, k].astype(F32)
        far_got[pair, band] = summed.astype(BF16)

    def go_far(pair):
        for k in sorted(range(1, n_far), key=lambda k: -min(k, n_far - k)):
            far_copy(pair, k).start()

    def sum_far(pair):
        for k in range(1, n_far):
            far_arrival(pair, k).wait_recv()
        summed = far_got[pair, 0].astype(F32)
        for k in range(1, n_far):
            summed += far_got[pair, k].astype(F32)
        total[pair] = (summed * inv_root).astype(BF16)
        for k in range(pair, n_near):
            ag_copy(pair, k).start()

    @pl.when(sums)
    def _():
        rs_got[1, me] = tiles[pl.ds(me * share, share)]
        sum_near(1)

    if n_space > 2 * near:
        @pl.when(odd == 1)
        def _():
            hear(1)

    @pl.when(sums)
    def _():
        go_far(1)
        sum_near(0)
        go_far(0)

    mean_out[...] = mean[...]
    prec_out[...] = prec[...]

    for i in (2, 3):
        arrived(i)

    @pl.when(has_prev)
    def _():
        act_out[...] = act_got[...]

    @pl.when(first_seg)
    def _():
        act_out[...] = jnp.zeros(act_out.shape, BF16)

    def planes(which, l_rows):
        put_r = lax.broadcasted_iota(jnp.int32, (256, 256), 0)
        put_c = lax.broadcasted_iota(jnp.int32, (256, 256), 1)
        weave = (put_c == 2 * (put_r % 128) + put_r // 128).astype(F32).astype(BF16)
        for i, pp in which:
            rows_i = [(1, i)] if pp == 0 else [(2, i), (0, i + 1)]
            lines = [None] * 6
            for qq in range(2):
                cols_j = [(1, 0)] if qq == 0 else [(2, 0), (0, 1)]
                left = jnp.concatenate(
                    [l_rows[3 * a + b] for a, _ in rows_i for b, _ in cols_j], axis=1
                )
                right = jnp.concatenate(
                    [
                        jnp.concatenate(
                            [shifted[ii, j + dj] for _, ii in rows_i for _, dj in cols_j], axis=0
                        )
                        for j in range(3)
                    ],
                    axis=1,
                )
                got = matmul(left, right).astype(BF16)
                for j in range(3):
                    line = got[:, 128 * j : 128 * j + 128]
                    lines[2 * j + qq] = jnp.concatenate([line[:32], line[32:]], axis=1)
            plane = matmul(jnp.concatenate(lines, axis=0), weave).astype(BF16)
            gin_out[2 * i + pp] = plane.reshape(6, 32, 256)

    inside = lax.broadcasted_iota(jnp.int32, (64, 128), 1) < 127

    def shift(i):
        for j in range(3):
            here = pg_got[i, j]
            moved = jnp.where(inside, pltpu.roll(here.astype(F32), 127, 1), 0.0)
            shifted[i, j, pl.ds(0, 64), :] = here
            shifted[i, j, pl.ds(64, 64), :] = moved.astype(BF16)
        shifted[i, 3] = jnp.zeros((128, 128), BF16)

    arrived(1)
    arrived(4)
    arrived(5)
    arrived(6)

    @pl.when(has_next)
    def _():
        @pl.when(jnp.logical_not(has_up))
        def _():
            pg_got[3] = jnp.zeros(pg_got.shape[1:], BF16)

        for i in range(4):
            shift(i)
        planes([(0, 0), (0, 1), (1, 0), (1, 1), (2, 0), (2, 1)], l_got)

    @pl.when(last_seg)
    def _():
        gin_out[...] = jnp.zeros(gin_out.shape, BF16)

    @pl.when(sums)
    def _():
        sum_far(1)
        sum_far(0)
        ag_got[pl.ds(me * share, share)] = total[1]

    for o in range(owners):
        @pl.when((me != o) | (odd == 0))
        def _():
            ag_arrival(o).wait_recv()

    scaled_out[...] = ag_got[:TAPS]

    for i in range(len(links)):
        sent(i)

    for o in range(owners):
        @pl.when((me != o) | (odd == 0))
        def _():
            near_copy(o).wait_send()

    @pl.when(sums)
    def _():
        for pair in range(2):
            for k in range(1, n_far):
                far_copy(pair, k).wait_send()
            for k in range(pair, n_near):
                ag_copy(pair, k).wait_send()


def deliver(
    act, gin, mean, prec, scaled, act_out, gin_out, mean_out, prec_out, mean_new, prec_new, done
):
    copies = []

    def send(src, dst, pieces):
        size = src.shape[0] // pieces
        for k in range(pieces):
            rows = pl.ds(size * k, size)
            copies.append(pltpu.make_async_copy(src.at[rows], dst.at[rows], done.at[len(copies)]))
            copies[-1].start()

    send(gin, gin_out, 3)
    send(act, act_out, 3)
    for t in range(TAPS):
        rows = pl.ds(16 * t, 16)
        step = scaled[t].astype(F32)
        fresh = 0.75 * prec[rows] + 0.25 * step * step
        prec_new[rows] = fresh
        mean_new[rows] = mean[rows] - 0.03 * step / (fresh + 0.1)
    send(prec_new, prec_out, 1)
    send(mean_new, mean_out, 1)
    for copy in copies:
        copy.wait()


def per_device(features, out_grad, weight_mean, weight_noise, precision):
    n_dp, n_seg, n_space = (lax.axis_size(a) for a in ("dp", "segment", "space"))
    near = 4 if n_space % 4 == 0 and n_space > 4 else 2
    n_near, n_far = n_dp * near, n_space // near
    share = -(-TAPS // n_near)
    feats = jnp.transpose(features[0, 0], (1, 2, 0, 3))
    og = jnp.transpose(out_grad[0, 0], (1, 2, 0, 3))
    mean, noise, prec = (
        w.reshape(TAPS * 16, 128) for w in (weight_mean, weight_noise, precision)
    )
    feats, og, mean, noise, prec = (
        pltpu.with_memory_space_constraint(v, pltpu.HBM) for v in (feats, og, mean, noise, prec)
    )
    vmem = pl.BlockSpec(memory_space=pltpu.VMEM)
    *results, scaled = pl.pallas_call(
        functools.partial(kernel, n_dp, n_seg, n_space, near, share),
        out_shape=[
            jax.ShapeDtypeStruct((3, 3, 64, 128), BF16),
            jax.ShapeDtypeStruct((6, 6, 32, 256), BF16),
            jax.ShapeDtypeStruct((TAPS * 16, 128), F32),
            jax.ShapeDtypeStruct((TAPS * 16, 128), F32),
            jax.ShapeDtypeStruct((TAPS, 16, 128), BF16),
        ],
        in_specs=[pl.BlockSpec(memory_space=pltpu.HBM)] * 5,
        out_specs=[vmem] * 5,
        scratch_shapes=[
            pltpu.VMEM((6, 6, 32, 256), BF16),
            pltpu.VMEM((3, 3, 64, 128), BF16),
            pltpu.VMEM((TAPS * 16, 128), F32),
            pltpu.VMEM((TAPS * 16, 128), F32),
            pltpu.VMEM((TAPS * 16, 128), F32),
            pltpu.VMEM((7, 7, 96, 128), BF16),
            pltpu.VMEM((GROUPS, 64, 128), F32),
            pltpu.VMEM((GROUPS * 128, 128), F32),
            pltpu.VMEM((9, 64, 128), BF16),
            pltpu.VMEM((9, 64, 128), BF16),
            pltpu.VMEM((6, 32, 256), BF16),
            pltpu.VMEM((3, 3, 64, 128), BF16),
            pltpu.VMEM((3, 3, 64, 128), BF16),
            pltpu.VMEM((3, 3, 64, 128), BF16),
            pltpu.VMEM((4, 3, 64, 128), BF16),
            pltpu.VMEM((4, 4, 128, 128), BF16),
            pltpu.VMEM((GROUPS, 64, 128), F32),
            pltpu.VMEM((64, 384), F32),
            pltpu.VMEM((n_near * share, 16, 128), BF16),
            pltpu.VMEM((2, n_near, share, 16, 128), BF16),
            pltpu.VMEM((2, n_far, share, 16, 128), BF16),
            pltpu.VMEM((2, share, 16, 128), BF16),
            pltpu.VMEM((n_near * share, 16, 128), BF16),
            pltpu.SemaphoreType.REGULAR((2, 2)),
            pltpu.SemaphoreType.DMA((5,)),
            pltpu.SemaphoreType.DMA((7,)),
            pltpu.SemaphoreType.DMA((7,)),
            pltpu.SemaphoreType.DMA((n_near,)),
            pltpu.SemaphoreType.DMA((2, n_near)),
            pltpu.SemaphoreType.DMA((2, n_far)),
            pltpu.SemaphoreType.DMA((2, n_far)),
            pltpu.SemaphoreType.DMA((2, n_near)),
            pltpu.SemaphoreType.DMA((n_near,)),
        ],
        compiler_params=pltpu.CompilerParams(
            collective_id=0, has_side_effects=True, vmem_limit_bytes=40 * 2**20
        ),
        cost_estimate=pl.CostEstimate(
            flops=600_000_000, bytes_accessed=3_000_000, transcendentals=200_000
        ),
    )(feats, og, mean, noise, prec)
    act, gin, mean_new, prec_new = pl.pallas_call(
        deliver,
        out_shape=[jax.ShapeDtypeStruct(v.shape, v.dtype) for v in results],
        in_specs=[vmem] * 5,
        out_specs=[pl.BlockSpec(memory_space=pltpu.HBM)] * 4,
        scratch_shapes=[
            pltpu.VMEM((TAPS * 16, 128), F32),
            pltpu.VMEM((TAPS * 16, 128), F32),
            pltpu.SemaphoreType.DMA((8,)),
        ],
        compiler_params=pltpu.CompilerParams(vmem_limit_bytes=4 * 2**20),
    )(*results, scaled)
    act = jnp.transpose(act, (2, 0, 1, 3))
    gin = jnp.transpose(gin, (2, 0, 1, 3))
    return (
        act[None, None],
        gin[None, None],
        mean_new.reshape(1, TAPS, 2048),
        prec_new.reshape(1, TAPS, 2048),
    )


def solution(mesh):
    in_specs = (
        P("dp", "segment", None, "space", None, None),
        P("dp", "segment", None, "space", None, None),
        P("segment", None, None),
        P("segment", None, None),
        P("segment", None, None),
    )
    out_specs = (
        P("dp", "segment", None, "space", None, None),
        P("dp", "segment", None, "space", None, None),
        P("segment", None, None),
        P("segment", None, None),
    )
    return jax.shard_map(
        per_device, mesh=mesh, in_specs=in_specs, out_specs=out_specs, check_vma=False
    )
```
